128 devices in a mesh: grp: 4 (over y), dev: 32 (over x, z, core).
Axes of the slice: x: 4, y: 4, z: 4, core: 2. Of those that a mesh axis runs over, the one named last changes fastest.
Arguments:
- points: bfloat16 [16384, 1024], P(('grp', 'dev')), may hold values from -6 to 6
- basis: bfloat16 [16384, 4096], P(('grp', 'dev')), may hold values from -0.75 to 0.75
- transfer_leaf: bfloat16 [16384, 4096], P(('grp', 'dev')), may hold values from -0.25 to 0.25
- transfer_mid: bfloat16 [2048, 4096], P(('grp', 'dev')), may hold values from -0.25 to 0.25
- near_blocks: bfloat16 [16384, 8, 4096], P(('grp', 'dev')), may hold values from -0.25 to 0.25
- near_src: int32 [16384, 8], P(('grp', 'dev')), may hold values from 0 to 16383, as said below
- leaf_coupling: bfloat16 [16384, 8, 4096], P(('grp', 'dev')), may hold values from -0.25 to 0.25
- far_leaf: int32 [16384, 8], P(('grp', 'dev')), may hold values from 0 to 16383, as said below
- mid_coupling: bfloat16 [2048, 16, 4096], P(('grp', 'dev')), may hold values from -0.1875 to 0.1875
- mid_target: int32 [2048, 16], P(('grp', 'dev')), may hold values from 0 to 2047, as said below
- top_coupling: bfloat16 [256, 16, 4096], P(('grp', 'dev')), may hold values from -0.1875 to 0.1875
- far_top: int32 [256, 16], P(('grp', 'dev')), may hold values from 0 to 255
Outputs:
- product: bfloat16 [16384, 1024], P(('grp', 'dev'))
The draws below stay inside these ranges and needn't reach their ends.
Inputs may be any that keep to these rules, and one draw needn't show every extreme that they name: `near_src`: each row i names leaves at most 128 away from i; the first entry is i itself, and the first leaf of every device block but the first names the leaf 128 before it. `far_leaf`: each row i names leaves at most 128 away from i; the first leaf of every device block but the first names the leaf 128 before it. `mid_target`: among the entries of one device's 16 rows, at most 4 name clusters of any one aligned block of 16 clusters; one such block receives exactly 4 from every device's rows.
All inputs are finite; a program needn't handle non-finite values.
Results may differ from the reference program's by a relative error of at most 0.0065.
Values may be sent and summed in bfloat16 or wider, within the bound.
A program may use at most 192 MiB of HBM per device.

```python
import jax
import jax.numpy as jnp
from jax import lax

LEAF = 64
RANK = 64
RHS = 16
NEAR = 8
FAR_LEAF = 8
FAR_MID = 16
FAR_TOP = 16
LEAF_DEV = 128
MID_DEV = 16
LEAVES = 16384
MIDS = 2048
TOPS = 256
N_GRP = 4
N_DEV = 32


def local_partners(key, count):
    own = jnp.arange(LEAVES, dtype=jnp.int32)[:, None]
    offset = jax.random.randint(key, (LEAVES, count), -LEAF_DEV, LEAF_DEV + 1)
    partner = jnp.clip(own + offset, 0, LEAVES - 1)
    column = jnp.arange(count, dtype=jnp.int32)[None, :]
    first_leaf = (own % LEAF_DEV == 0) & (own >= LEAF_DEV)
    partner = jnp.where(first_leaf & (column == count - 1), own - LEAF_DEV, partner)
    return partner


def draw_near_src(key, part):
    key = jax.random.fold_in(key, 5)
    partner = local_partners(key, NEAR)
    own = jnp.arange(LEAVES, dtype=jnp.int32)[:, None]
    column = jnp.arange(NEAR, dtype=jnp.int32)[None, :]
    return jnp.where(column == 0, own, partner).astype(jnp.int32)


def draw_far_leaf(key, part):
    key = jax.random.fold_in(key, 7)
    return local_partners(key, FAR_LEAF).astype(jnp.int32)


def draw_mid_target(key, part):
    key = jax.random.fold_in(key, 11)
    blocks = MIDS // MID_DEV
    pairs = MID_DEV * FAR_MID
    cap = 2 * pairs // blocks
    quarter = blocks // 4
    half = pairs // 2
    busy = jax.random.randint(jax.random.fold_in(key, 0), (), 0, blocks)

    def one_block(index):
        sub = jax.random.fold_in(key, index + 1)
        first_key, order_key, local_key = jax.random.split(sub, 3)
        others = (busy + 1 + jax.random.permutation(first_key, blocks - 1)) % blocks
        order = jnp.concatenate([busy[None], others])
        slot = jnp.arange(pairs, dtype=jnp.int32)
        early = order[jnp.minimum(slot // cap, blocks - 1)]
        later = order[quarter + (slot - half) % (blocks - quarter)]
        dest = jnp.where(slot < half, early, later)
        dest = dest[jax.random.permutation(order_key, pairs)]
        local = jax.random.randint(local_key, (pairs,), 0, MID_DEV)
        return (dest * MID_DEV + local).reshape(MID_DEV, FAR_MID)
    return jax.vmap(one_block)(jnp.arange(blocks, dtype=jnp.int32)).reshape(MIDS, FAR_MID).astype(jnp.int32)


def with_ends(values, stream_key, low, high):
    longest = values.shape.index(max(values.shape))
    spots = []
    for shift in (0, 1):
        where = [jax.random.randint(jax.random.fold_in(stream_key, axis), (), 0, length) for axis, length in enumerate(values.shape)]
        where[longest] = (where[longest] + shift) % values.shape[longest]
        spots.append(tuple(where))
    return values.at[spots[0]].set(low).at[spots[1]].set(high)


def level_of(rng, shape, cuts, least, top_value):
    gain, own = 1.0, jax.random.fold_in(rng, 6)
    for dim, shards_of in cuts:
        draws = jnp.exp(jax.random.uniform(jax.random.fold_in(own, dim), (shards_of,), jnp.float32, least / len(cuts), top_value / len(cuts)))
        gain = gain * jnp.repeat(draws, shape[dim] // shards_of).reshape([-1 if axis == dim else 1 for axis in range(len(shape))])
    return gain


def noise(key, extent, deviation, limit, shards=(), held_as=jnp.bfloat16):
    drawn = jax.random.normal(key, extent, jnp.float32) * deviation
    if len(shards) > 0:
        drawn = level_of(key, extent, shards, -0.22, 0.18) * drawn
    return jnp.clip(drawn, min=-limit, max=limit).astype(held_as)


def setup_inputs(seed: int = 0) -> dict:
    key_of = jax.random.split(jax.random.key(seed), 13)
    points = noise(key_of[0], (LEAVES, RHS * LEAF), 1.0, 6.0, ((0, 128),))
    basis = noise(key_of[1], (LEAVES, LEAF * RANK), LEAF ** -0.5, 0.75, ((0, 128),))
    transfer_leaf = noise(key_of[2], (LEAVES, RANK * RANK), (8 * RANK) ** -0.5, 0.25, ((0, 128),))
    transfer_mid = noise(key_of[3], (MIDS, RANK * RANK), (8 * RANK) ** -0.5, 0.25, ((0, 128),))
    near_blocks = noise(key_of[4], (LEAVES, NEAR, LEAF * LEAF), (NEAR * LEAF) ** -0.5, 0.25, ((0, 128),))
    near_src = draw_near_src(jax.random.fold_in(key_of[12], 71), 0)
    leaf_coupling = noise(key_of[6], (LEAVES, FAR_LEAF, RANK * RANK), (FAR_LEAF * RANK) ** -0.5, 0.25, ((0, 128),))
    far_leaf = draw_far_leaf(jax.random.fold_in(key_of[12], 71), 0)
    mid_coupling = noise(key_of[8], (MIDS, FAR_MID, RANK * RANK), (FAR_MID * RANK) ** -0.5, 0.1875, ((0, 128),))
    mid_target = draw_mid_target(jax.random.fold_in(key_of[12], 71), 0)
    top_coupling = noise(key_of[10], (TOPS, FAR_TOP, RANK * RANK), (FAR_TOP * RANK) ** -0.5, 0.1875, ((0, 128),))
    far_top = with_ends(jax.random.randint(key_of[11], (TOPS, FAR_TOP), 0, TOPS), jax.random.fold_in(key_of[11], 1), 0, TOPS - 1).astype(jnp.int32)
    return dict(points=points, basis=basis, transfer_leaf=transfer_leaf, transfer_mid=transfer_mid, near_blocks=near_blocks, near_src=near_src, leaf_coupling=leaf_coupling, far_leaf=far_leaf, mid_coupling=mid_coupling, mid_target=mid_target, top_coupling=top_coupling, far_top=far_top)


def reference(points, basis, transfer_leaf, transfer_mid, near_blocks, near_src, leaf_coupling, far_leaf, mid_coupling, mid_target, top_coupling, far_top):
    f32 = jnp.float32
    bf = jnp.bfloat16
    nblk = N_GRP * N_DEV
    xs = points.reshape(LEAVES, RHS, LEAF)
    vecs = basis.reshape(LEAVES, LEAF, RANK)
    leaf_coef = jnp.einsum('irp,ipk->irk', xs.astype(f32), vecs.astype(f32)).astype(bf)
    tleaf = transfer_leaf.reshape(MIDS, 8, RANK, RANK)
    mid_coef = jnp.einsum('qckm,qcrk->qrm', tleaf.astype(f32), leaf_coef.reshape(MIDS, 8, RHS, RANK).astype(f32)).astype(bf)
    tmid = transfer_mid.reshape(TOPS, 8, RANK, RANK)
    top_coef = jnp.einsum('tcmn,tcrm->trn', tmid.astype(f32), mid_coef.reshape(TOPS, 8, RHS, RANK).astype(f32)).astype(bf)

    def leaf_block(args):
        coupling, index = args
        picked = leaf_coef[index].astype(f32)
        return jnp.einsum('ijab,ijrb->ira', coupling.reshape(-1, FAR_LEAF, RANK, RANK).astype(f32), picked)

    leaf_far = lax.map(leaf_block, (leaf_coupling.reshape(nblk, LEAF_DEV, FAR_LEAF, RANK * RANK), far_leaf.reshape(nblk, LEAF_DEV, FAR_LEAF))).reshape(LEAVES, RHS, RANK)

    def mid_block(args):
        coupling, coef = args
        return jnp.einsum('sjab,srb->sjra', coupling.reshape(-1, FAR_MID, RANK, RANK).astype(f32), coef.astype(f32)).astype(bf)

    contrib = lax.map(mid_block, (mid_coupling.reshape(nblk, MID_DEV, FAR_MID, RANK * RANK), mid_coef.reshape(nblk, MID_DEV, RHS, RANK)))
    mid_far = jnp.zeros((MIDS, RHS, RANK), f32).at[mid_target.reshape(-1)].add(contrib.reshape(-1, RHS, RANK).astype(f32))

    top_picked = top_coef[far_top].astype(f32)
    top_far = jnp.einsum('tjab,tjrb->tra', top_coupling.reshape(TOPS, FAR_TOP, RANK, RANK).astype(f32), top_picked)
    top_field = top_far.astype(bf)
    mid_field = (mid_far + jnp.einsum('tcmn,trn->tcrm', tmid.astype(f32), top_field.astype(f32)).reshape(MIDS, RHS, RANK)).astype(bf)
    leaf_field = (leaf_far + jnp.einsum('qckm,qrm->qcrk', tleaf.astype(f32), mid_field.astype(f32)).reshape(LEAVES, RHS, RANK)).astype(bf)

    def out_block(args):
        blocks, index, vblock, field = args
        picked = xs[index].astype(f32)
        near_part = jnp.einsum('ijpu,ijru->irp', blocks.reshape(-1, NEAR, LEAF, LEAF).astype(f32), picked)
        far_part = jnp.einsum('ipk,irk->irp', vblock.astype(f32), field.astype(f32))
        return near_part + far_part

    total = lax.map(out_block, (near_blocks.reshape(nblk, LEAF_DEV, NEAR, LEAF * LEAF), near_src.reshape(nblk, LEAF_DEV, NEAR), vecs.reshape(nblk, LEAF_DEV, LEAF, RANK), leaf_field.reshape(nblk, LEAF_DEV, RHS, RANK)))
    return total.reshape(LEAVES, RHS * LEAF).astype(bf)
```

```python
import functools

import jax
import jax.numpy as jnp
from jax import lax
from jax.experimental import pallas as pl
from jax.experimental.pallas import tpu as pltpu
from jax.sharding import PartitionSpec as P

F32 = jnp.float32
BF = jnp.bfloat16
AXES = ("grp", "dev")
GROUPS = 16
DEVICES = 128
LEAVES = 16
STEPS = 128 // LEAVES


def dot(a, b):
    return jnp.dot(a, b, preferred_element_type=F32)


def dot_nt(a, b):
    return lax.dot_general(a, b, (((1,), (1,)), ((), ())), preferred_element_type=F32)


def iota(shape, dim):
    return lax.broadcasted_iota(jnp.int32, shape, dim)


def ones_where(condition):
    return jnp.where(condition, 1.0, 0.0).astype(BF)


def low_lanes(shape):
    return iota(shape, len(shape) - 1) < 64


def spread(half):
    shape = (64, 256)
    return ones_where(iota(shape, 0) == 2 * (iota(shape, 1) // 8) + half)


def gather_back(half):
    shape = (128, 256)
    return ones_where(iota(shape, 0) % 64 == 2 * (iota(shape, 1) // 8) + half)


def own_child():
    shape = (128, 256)
    return iota(shape, 0) // 16 == iota(shape, 1) % 8


def fold_halves(first, second):
    v = jnp.where(low_lanes(first.shape), first, second)
    return v + pltpu.roll(v, 64, 1)


def both_halves(v):
    low = low_lanes(v.shape)
    zero = jnp.zeros_like(v)
    return jnp.concatenate([jnp.where(low, v, zero), jnp.where(low, zero, v)], axis=0)


def spread_sources(dst, n, v):
    low = low_lanes(v.shape)
    zero = jnp.zeros_like(v)
    count = v.shape[0] // 16
    dst[n : n + count, 0:16, :] = jnp.where(low, v, zero).reshape(count, 16, 128)
    dst[n : n + count, 16:32, :] = jnp.where(low, zero, v).reshape(count, 16, 128)


def up_pass(loads, points_ready, coefs_ready, pt, basis, tl, tm, xp, cp, mc, tops, xd, cd):
    e01 = jnp.concatenate([spread(0), spread(1)], axis=1)
    shape = (2048, 512)
    own = (iota(shape, 0) // 16) % 8 == iota(shape, 1) % 8
    shape = (128, 64)
    pick = ones_where(
        (iota(shape, 0) // 16 == iota(shape, 1) % 8)
        & ((iota(shape, 0) % 16) // 2 == iota(shape, 1) // 8)
    )
    shape = (128, 128)
    fold = ones_where(iota(shape, 0) % 64 == iota(shape, 1) % 64)
    parity = iota(shape, 1) // 64 == iota(shape, 0) % 2

    def expanded(v):
        n = v.shape[0]
        return jnp.where(own[:n], dot(v[:, :64], e01), 0.0)

    def parents(v, blocks):
        n = len(blocks)
        lhs = jnp.sum(expanded(v).reshape(n, 8, 16, 512), axis=1).astype(BF)
        out = []
        for k in range(n):
            d = dot(jnp.concatenate([lhs[k, :, :256], lhs[k, :, 256:]], axis=0), blocks[k])
            out.append(fold_halves(d[:16], d[16:]).astype(BF))
        return jnp.concatenate(out, axis=0)

    loads[0].wait()
    a = [jnp.where(parity, dot(pick, pt[k]), 0.0).astype(BF) for k in range(GROUPS)]
    x = dot(jnp.concatenate(a, axis=0), fold).astype(BF)
    low = low_lanes((1024, 128))
    xp[...] = jnp.where(low, x[:1024], x[1024:])
    points_ready()
    spread_sources(xd, 128, x)
    wide = expanded(x).astype(BF)
    loads[1].wait()
    coef = []
    for k in range(GROUPS):
        w = wide[128 * k : 128 * (k + 1)]
        c = dot(jnp.concatenate([w[:, :256], w[:, 256:]], axis=0), basis[k])
        coef.append(fold_halves(c[:128], c[128:]).astype(BF))
    coef = jnp.concatenate(coef, axis=0)
    cp[...] = jnp.where(low, coef[:1024], coef[1024:])
    coefs_ready()
    spread_sources(cd, 128, coef)
    loads[2].wait()
    mc[...] = parents(coef, [tl[k] for k in range(GROUPS)])
    loads[3].wait()
    both = parents(mc[...], [tm[0], tm[1]])
    tops[...] = jnp.where(low_lanes((16, 128)), both[:16], both[16:])


def regroup():
    shape = (256, 256)
    row, col = iota(shape, 0), iota(shape, 1)
    return ones_where((row // 32 == col % 8) & (row % 32 == col // 8))


def widen(half):
    shape = (32, 128)
    return ones_where(iota(shape, 1) % 64 == 2 * iota(shape, 0) + half)


def blocks_times(sources, regrouped):
    lhs = jnp.concatenate(sources, axis=1)
    rhs = jnp.concatenate([regrouped[32 * j : 32 * (j + 1)] for j in range(8)], axis=1)
    return dot_nt(lhs, rhs)


def place_messages(cm, mt, mc, msgs, cb):
    rep = iota((8, 8, 128), 2) // 32

    def mid_step(s, carry):
        y = both_halves(mc[pl.ds(pl.multiple_of(s * 16, 16), 16), :])
        y = jnp.concatenate([y] * 4, axis=0)
        zero = jnp.zeros_like(y)
        top = jnp.concatenate([y, zero], axis=1)
        low = jnp.concatenate([zero, y], axis=1)
        block = jnp.concatenate([cm[s, 0:256, :], cm[s, 256:512, :]], axis=1)
        r = dot_nt(block, jnp.concatenate([top, low], axis=0))
        parts = []
        for jh in range(2):
            b = r[:, 128 * jh : 128 * jh + 128].reshape(8, 4, 8, 128)
            q = b[:, 0]
            for k in range(1, 4):
                q = jnp.where(rep == k, b[:, k], q)
            parts.append(q)
        cb[:, pl.ds(pl.multiple_of(s * 16, 16), 16), :] = jnp.concatenate(parts, axis=1).astype(BF)
        return carry

    lax.fori_loop(0, GROUPS, mid_step, 0, unroll=4)

    target = mt[...]
    owner = target // 16
    parts = (owner // 32, (owner // 8) % 4, (owner // 2) % 4, owner % 2, target % 16)
    parts = jnp.concatenate(parts, axis=0).astype(F32).astype(BF)
    shape = (16, 256)
    along = ones_where(iota(shape, 1) % 16 == iota(shape, 0))
    mine = iota(shape, 1) // 16 == iota(shape, 0)
    parts = dot(parts, along)
    y, x, z, c, local = [
        jnp.sum(jnp.where(mine, parts[16 * k : 16 * k + 16], 0.0), axis=0, keepdims=True)
        for k in range(5)
    ]
    shape = (128, 256)
    onehot = iota(shape, 0).astype(F32) == 32.0 * y + 8.0 * x + 2.0 * z + c
    shape = (256, 256)
    earlier = ones_where(iota(shape, 0) < iota(shape, 1))
    rank = jnp.where(onehot, dot(ones_where(onehot), earlier), 0.0)
    rank = jnp.sum(rank, axis=0, keepdims=True)

    plans = (
        (0, 3, 2.0 * x + c, 4.0 * z + y),
        (3, 3, 2.0 * z + c, 4.0 * y + x),
        (6, 2, 2.0 * y + c, 4.0 * x + z),
    )
    for msg, (first, count, stop, rest) in zip(msgs, plans):
        at = 4.0 * rest + rank
        slot = iota((512, 256), 0).astype(F32)
        place = ones_where(slot == 64.0 * stop + at)
        wide = jnp.concatenate([cb[first + k] for k in range(count)], axis=1)
        wide = dot(place, wide).astype(BF)
        for k in range(count):
            rows = wide[:, 128 * k : 128 * k + 128].reshape(8, 64, 128)
            msg[:, 64 * k : 64 * k + 64, :] = rows
        shape = (128, 256)
        to_stop = (iota(shape, 0) // 16).astype(F32) == stop
        value = jnp.where(to_stop, local + 1.0, 0.0).astype(BF)
        lane = ones_where((iota(shape, 0) % 64).astype(F32) == at)
        label = dot_nt(value, lane) - 1.0
        msg[:, 64 * count : 64 * count + 16, :] = label.astype(BF).reshape(8, 16, 128)


def sum_messages(count, landed, sums):
    shape = (16, 128)
    first = iota(shape, 1) < 64
    labels = pl.ds(64 * count, 16)
    lab = [
        jnp.where(first, landed[2 * q, labels, :], landed[2 * q + 1, labels, :])
        for q in range(4)
    ]
    lab = jnp.concatenate(lab, axis=1).astype(F32)
    shape = (16, 512)
    hit = lab == iota(shape, 0).astype(F32)
    to = (iota(shape, 1) // 4) % 16
    lhs = jnp.concatenate([ones_where(hit & (to == n)) for n in range(16)], axis=0)
    parts = [landed[:, 64 * k : 64 * k + 64, :].reshape(512, 128) for k in range(count)]
    total = dot(lhs, jnp.concatenate(parts, axis=1)).astype(BF)
    sums[...] = total.reshape(4, 64, 128 * count)


def near_kernel(
    near_idx, far_idx, ft, mt, near_in, far_in, pt_in, basis_in, tl_in, tm_in, cm_in, tc_in,
    out,
    near, far, near_sum, far_sum, xd, cd, xland, cland, bw, cm, cb, pt, basis, tl, tm, tc, xp, cp, mc, tops,
    all_tops,
    msg_a, msg_b, msg_c, land_a, land_b, land_c,
    sum_a, sum_b, sum_c, next_a, next_b, next_c, part_a, part_b, part_c,
    sums_a, sums_b, sums_c, send, recv, here, fetch,
):
    y = lax.axis_index("grp")
    dev = lax.axis_index("dev")
    x, z, c = dev // 8, (dev // 2) % 4, dev % 2
    me = y * 32 + dev
    right = lax.rem(me + 1, DEVICES)
    left = lax.rem(me + DEVICES - 1, DEVICES)
    mesh = pl.DeviceIdType.MESH

    def remote(src, dst, n, device):
        return pltpu.make_async_remote_copy(
            src_ref=src,
            dst_ref=dst,
            send_sem=send.at[n],
            recv_sem=recv.at[n],
            device_id=device,
            device_id_type=mesh,
        )

    def at_x(k):
        return (y, lax.rem(x + k, 4) * 8 + z * 2 + c)

    def at_y(k):
        return (lax.rem(y + k, 4), dev)

    def at_z(k):
        return (y, x * 8 + lax.rem(z + k, 4) * 2 + c)

    def at_xc(k):
        m = lax.rem(x * 2 + c + k, 8)
        return (y, (m // 2) * 8 + z * 2 + m % 2)

    def at_yc(k):
        m = lax.rem(y * 2 + c + k, 8)
        return (m // 2, x * 8 + z * 2 + m % 2)

    def at_zc(k):
        return (y, x * 8 + lax.rem(z * 2 + c + k, 8))

    def halos(n):
        src, dst = ((xp, xland), (cp, cland))[n]
        return [
            remote(src, dst.at[k], 2 * n + k, (to // 32, to % 32))
            for k, to in enumerate((right, left))
        ]

    def tops_to(n):
        if n == 0:
            return [remote(tops, all_tops.at[c, y, z, x], 3 + k, at_x(k)) for k in range(1, 4)]
        if n == 1:
            block = all_tops.at[c, y, z]
            return [remote(block, block, 6 + k, at_z(k)) for k in range(1, 4)]
        if n == 2:
            block = all_tops.at[c, y]
            return [remote(block, block, 9 + k, at_y(k)) for k in range(1, 4)]
        block = all_tops.at[c]
        return [remote(block, block, 13, (y, x * 8 + z * 2 + 1 - c))]

    plans = (
        (3, (x, z, y), (at_xc, at_z, at_y), msg_a, land_a, sum_a, next_a, part_a, sums_a),
        (3, (z, y, x), (at_zc, at_y, at_x), msg_b, land_b, sum_b, next_b, part_b, sums_b),
        (2, (y, x, z), (at_yc, at_x, at_z), msg_c, land_c, sum_c, next_c, part_c, sums_c),
    )

    def first_hop(n):
        _, (a, _, _), (to, _, _), msg, land = plans[n][:5]
        own = a * 2 + c
        return [
            remote(msg.at[lax.rem(own + k, 8)], land.at[own], 13 + 7 * n + k, to(k))
            for k in range(1, 8)
        ]

    def second_hop(n):
        _, (_, a, _), (_, to, _), _, _, src, dst = plans[n][:7]
        return [
            remote(src.at[lax.rem(a + k, 4)], dst.at[a], 34 + 3 * n + k, to(k))
            for k in range(1, 4)
        ]

    def third_hop(n):
        _, (_, _, a), (_, _, to), _, _, _, _, src, dst = plans[n]
        return [
            remote(src.at[lax.rem(a + k, 4)], dst.at[a], 43 + 3 * n + k, to(k))
            for k in range(1, 4)
        ]

    def own_first(n):
        own = plans[n][1][0] * 2 + c
        return pltpu.make_async_copy(plans[n][3].at[own], plans[n][4].at[own], here.at[n])

    def own_third(n):
        own = plans[n][1][2]
        return pltpu.make_async_copy(plans[n][7].at[own], plans[n][8].at[own], here.at[3 + n])

    def own_tops():
        return pltpu.make_async_copy(tops, all_tops.at[c, y, z, x], here.at[6])

    def chunk(src, dst, base, n):
        part = pl.ds(n * LEAVES, LEAVES)
        return pltpu.make_async_copy(src.at[part], dst.at[part], fetch.at[base + n])

    def start(copies):
        for copy in copies:
            copy.start()

    def arrive(copies):
        for copy in copies:
            copy.wait_recv()

    low = low_lanes((1024, 128))

    def unpack(dst, part, n):
        shape = (128, 128)
        swap = ones_where((iota(shape, 0) + 64) % 128 == iota(shape, 1))
        v = part[...]
        w = dot(v, swap).astype(BF)
        for h, (lo, hi) in enumerate(((v, w), (w, v))):
            at = n * 128 + h * 64
            zero = jnp.zeros_like(v)
            dst[at : at + 64, 0:16, :] = jnp.where(low, lo, zero).reshape(64, 16, 128)
            dst[at : at + 64, 16:32, :] = jnp.where(low, zero, hi).reshape(64, 16, 128)

    pairs = (
        (pt_in, pt), (basis_in, basis), (tl_in, tl), (tm_in, tm), (cm_in, cm), (tc_in, tc),
    )
    loads = [
        pltpu.make_async_copy(src, dst, here.at[7 + n]) for n, (src, dst) in enumerate(pairs)
    ]
    start(loads)
    barrier = pltpu.get_barrier_semaphore()

    def greet(device):
        pl.semaphore_signal(barrier, inc=1, device_id=device, device_id_type=mesh)

    for to in (right, left):
        greet((to // 32, to % 32))
    for k in range(1, 8):
        greet(at_xc(k))
        greet(at_yc(k))
        greet(at_zc(k))

    def points_ready():
        pl.semaphore_wait(barrier, 23)
        start(halos(0))
        start([chunk(near_in, near, 0, n) for n in range(STEPS)])

    def coefs_ready():
        start(halos(1))
        start([chunk(far_in, far, STEPS, n) for n in range(STEPS)])

    up_pass(loads, points_ready, coefs_ready, pt, basis, tl, tm, xp, cp, mc, tops, xd, cd)
    start(tops_to(0))
    own_tops().start()
    loads[4].wait()
    loads[5].wait()
    place_messages(cm, mt, mc, (msg_a, msg_b, msg_c), cb)
    for copies in zip(first_hop(0), first_hop(1), first_hop(2)):
        start(copies)
    for n in range(3):
        own_first(n).start()
    bw[0] = gather_back(0)
    bw[1] = gather_back(1)
    arrive(halos(0))
    unpack(xd, xland.at[0], 0)
    unpack(xd, xland.at[1], 2)

    anchor = (me - 1) * 128

    def work(g, idx, blocks, src, out):
        pair = (iota((32, 256), 1) % 8) // 2
        even = ones_where(iota((1, 16, 128), 1) % 2 == 0)
        odd = ones_where(iota((1, 16, 128), 1) % 2 == 1)
        for i in range(LEAVES):
            found = [src[jnp.clip(idx[j, g * LEAVES + i] - anchor, 0, 383)] for j in range(8)]
            lhs = [jnp.concatenate(found[j : j + 2], axis=1) for j in range(0, 8, 2)]
            block = blocks[g * LEAVES + i].reshape(16, 16, 128)
            rhs = jnp.concatenate([block * even, block * odd], axis=2).reshape(256, 256)
            z = dot_nt(jnp.concatenate(lhs, axis=0), rhs)
            o = z[0:32]
            for j in range(1, 4):
                o = jnp.where(pair == j, z[32 * j : 32 * j + 32], o)
            rows = pl.ds(pl.multiple_of((g * LEAVES + i) * 16, 16), 16)
            out[0, rows, :] = o[:16]
            out[1, rows, :] = o[16:]

    def near_step(g, carry):
        @pl.when(g == 1)
        def _():
            own_tops().wait()
            arrive(tops_to(0))
            start(tops_to(1))

        @pl.when(g == 3)
        def _():
            arrive(tops_to(1))
            start(tops_to(2))

        @pl.when(g == STEPS - 1)
        def _():
            arrive(tops_to(2))
            start(tops_to(3))

        chunk(near_in, near, 0, g).wait()
        work(g, near_idx, near, xd, near_sum)
        return carry

    lax.fori_loop(0, STEPS, near_step, 0)
    for n in range(3):
        own_first(n).wait()
        arrive(first_hop(n))
    arrive(halos(1))
    for n in range(3):
        sum_messages(plans[n][0], plans[n][4], plans[n][5])
    for n in range(3):
        start(second_hop(n))
    unpack(cd, cland.at[0], 0)
    unpack(cd, cland.at[1], 2)

    def far_step(g, carry):
        @pl.when(g == 4)
        def _():
            for n in range(3):
                arrive(second_hop(n))
            for n in range(3):
                at, own, got, dst = plans[n][1][1], plans[n][5], plans[n][6], plans[n][7]
                total = own[at].astype(F32)
                for k in range(1, 4):
                    total = total + got[lax.rem(at + k, 4)].astype(F32)
                dst[...] = total.astype(BF).reshape(dst.shape)
            for n in range(3):
                start(third_hop(n))
                own_third(n).start()

        chunk(far_in, far, STEPS, g).wait()
        work(g, far_idx, far, cd, far_sum)
        return carry

    lax.fori_loop(0, STEPS, far_step, 0)
    arrive(tops_to(3))
    for n in range(3):
        own_third(n).wait()
        arrive(third_hop(n))
    b0, b1 = bw[0], bw[1]
    down = from_tops(ft, all_tops, tc, tm, b0, b1)
    fields = (from_mids((sums_a, sums_b, sums_c)) + down).astype(BF)
    leaves_out(fields, tl, basis, near_sum, far_sum, b0, b1, out)
    sent = [halos(0), halos(1)] + [tops_to(n) for n in range(4)]
    for n in range(3):
        sent += [first_hop(n), second_hop(n), third_hop(n)]
    for copies in sent:
        for copy in copies:
            copy.wait_send()


def converted(first, second, b0, b1):
    first = jnp.concatenate(first, axis=0)
    second = jnp.concatenate(second, axis=0)
    return dot_nt(first, b0) + dot_nt(second, b1)


def for_children(field, t):
    own = own_child()
    d = dot_nt(both_halves(field), t)
    return [
        jnp.where(own, jnp.concatenate([d[16 * k : 16 * k + 16]] * 8, axis=0), 0.0)
        for k in range(2)
    ]


def from_tops(ft, all_tops, tc, tm, b0, b1):
    w0, w1 = widen(0), widen(1)
    order = regroup()
    shape = (128, 128)
    fold = ones_where(iota(shape, 0) % 64 == iota(shape, 1) % 64)
    shape = (16, 128)
    half = iota(shape, 1) // 64
    found = []
    for n in range(32):
        top = ft[n // 16, n % 16]
        dev = top // 2
        y, x, z, c = dev // 32, (dev // 8) % 4, (dev // 2) % 4, dev % 2
        v = all_tops[c, y, z, x]
        found.append(jnp.where(half == top % 2, v, jnp.zeros_like(v)))
    found = dot(jnp.concatenate(found, axis=0), fold).astype(BF)
    fields = []
    for t in range(2):
        total = jnp.zeros((32, 32), F32)
        for jh in range(2):
            regrouped = dot(order, tc[t, jh * 256 : (jh + 1) * 256, :]).astype(BF)
            first = (t * 16 + jh * 8) * 16
            srcs = [both_halves(found[first + 16 * j : first + 16 * (j + 1)]) for j in range(8)]
            total = total + blocks_times(srcs, regrouped)
        total = total.astype(BF)
        fields.append((dot(total[:16], w0) + dot(total[16:], w1)).astype(BF))
    first, second = zip(*[for_children(fields[t], tm[t]) for t in range(2)])
    return converted([v.astype(BF) for v in first], [v.astype(BF) for v in second], b0, b1)


def from_mids(parts):
    wide = []
    for part in parts:
        total = part[0].astype(F32)
        for k in range(1, 4):
            total = total + part[k].astype(F32)
        wide.append(total)
    wide = jnp.concatenate(wide, axis=1).astype(BF)
    shape = (256, 16)
    repeat = ones_where(iota(shape, 0) // 16 == iota(shape, 1))
    shape = (256, 1024)
    keep = iota(shape, 1) % 16 == iota(shape, 0) % 16
    m = jnp.where(keep, dot(repeat, wide), 0.0).astype(BF)
    shape = (1024, 128)
    to_m = ones_where(iota(shape, 0) // 16 == iota(shape, 1) % 64)
    return dot(m, to_m)


def leaves_out(fields, tl, basis, near_sum, far_sum, b0, b1, out):
    own = own_child()
    shape = (64, 128)
    row, col = iota(shape, 0), iota(shape, 1)
    same = row % 8 == col // 16
    pick0 = ones_where(same & (col % 16 == 2 * (row // 8)))
    pick1 = ones_where(same & (col % 16 == 2 * (row // 8) + 1))
    low = low_lanes(shape)
    first, second = [], []
    for k in range(GROUPS):
        m0, m1 = for_children(fields[16 * k : 16 * k + 16], tl[k])
        rows = slice(128 * k, 128 * k + 128)
        first.append((m0 + far_sum[0, rows, :]).astype(BF))
        second.append((m1 + far_sum[1, rows, :]).astype(BF))
    leaf = converted(first, second, b0, b1).astype(BF)
    first, second = [], []
    for k in range(GROUPS):
        rows = slice(128 * k, 128 * k + 128)
        z = dot_nt(both_halves(leaf[rows]), basis[k])
        first.append((jnp.where(own, z[:128], 0.0) + near_sum[0, rows, :]).astype(BF))
        second.append((jnp.where(own, z[128:], 0.0) + near_sum[1, rows, :]).astype(BF))
    total = converted(first, second, b0, b1).astype(BF)
    for k in range(GROUPS):
        v = total[128 * k : 128 * (k + 1)]
        out[k] = jnp.where(low, dot(pick0, v), dot(pick1, v)).astype(BF)


def as_tiles(a):
    n = a.shape[0]
    return a.reshape(n, 8, 32, 128).transpose(0, 2, 1, 3).reshape(n, 256, 128)


VMEM = pl.BlockSpec(memory_space=pltpu.VMEM)
ANY = pl.BlockSpec(memory_space=pl.ANY)
SMEM = pl.BlockSpec(memory_space=pltpu.SMEM)
LIMIT = 56 * 1024 * 1024


def body(
    points,
    basis,
    transfer_leaf,
    transfer_mid,
    near_blocks,
    near_src,
    leaf_coupling,
    far_leaf,
    mid_coupling,
    mid_target,
    top_coupling,
    far_top,
):
    pt = points.reshape(16, 8, 8, 128).transpose(0, 2, 1, 3).reshape(16, 64, 128)
    bt = as_tiles(basis.reshape(16, 8, 4096))
    tl = as_tiles(transfer_leaf.reshape(16, 8, 4096))
    tm = as_tiles(transfer_mid.reshape(2, 8, 4096))
    cm = as_tiles(mid_coupling.reshape(32, 8, 4096)).reshape(16, 512, 128)
    tc = as_tiles(top_coupling.reshape(4, 8, 4096)).reshape(2, 512, 128)
    nb = as_tiles(near_blocks)
    fb = as_tiles(leaf_coupling)

    lanes = (384, 384, 256)
    out = pl.pallas_call(
        near_kernel,
        out_shape=jax.ShapeDtypeStruct((16, 64, 128), BF),
        in_specs=[SMEM] * 3 + [VMEM] + [ANY] * 8,
        out_specs=VMEM,
        scratch_shapes=[
            pltpu.VMEM((128, 256, 128), BF),
            pltpu.VMEM((128, 256, 128), BF),
            pltpu.VMEM((2, 2048, 256), F32),
            pltpu.VMEM((2, 2048, 256), F32),
            pltpu.VMEM((384, 32, 128), BF),
            pltpu.VMEM((384, 32, 128), BF),
            pltpu.VMEM((2, 1024, 128), BF),
            pltpu.VMEM((2, 1024, 128), BF),
            pltpu.VMEM((2, 128, 256), BF),
            pltpu.VMEM((16, 512, 128), BF),
            pltpu.VMEM((8, 256, 128), BF),
            pltpu.VMEM((16, 64, 128), BF),
            pltpu.VMEM((16, 256, 128), BF),
            pltpu.VMEM((16, 256, 128), BF),
            pltpu.VMEM((2, 256, 128), BF),
            pltpu.VMEM((2, 512, 128), BF),
            pltpu.VMEM((1024, 128), BF),
            pltpu.VMEM((1024, 128), BF),
            pltpu.VMEM((256, 128), BF),
            pltpu.VMEM((16, 128), BF),
            pltpu.VMEM((2, 4, 4, 4, 16, 128), BF),
        ]
        + [pltpu.VMEM((8, n // 2 + 16, 128), BF) for n in lanes] * 2
        + [pltpu.VMEM((4, 64, n), BF) for n in lanes] * 2
        + [pltpu.VMEM((4, 16, n), BF) for n in lanes] * 2
        + [
            pltpu.SemaphoreType.DMA((53,)),
            pltpu.SemaphoreType.DMA((53,)),
            pltpu.SemaphoreType.DMA((13,)),
            pltpu.SemaphoreType.DMA((2 * STEPS,)),
        ],
        compiler_params=pltpu.CompilerParams(
            vmem_limit_bytes=LIMIT, collective_id=0, has_side_effects=True
        ),
        name="whole",
    )(near_src.T, far_leaf.T, far_top, mid_target, nb, fb, pt, bt, tl, tm, cm, tc)
    return out.reshape(16, 8, 8, 128).transpose(0, 2, 1, 3).reshape(128, 1024)


def solution(mesh):
    both = P(AXES, None)
    three = P(AXES, None, None)
    return jax.shard_map(
        body,
        mesh=mesh,
        in_specs=(
            both, both, both, both, three, both, three, both, three, both, three, both,
        ),
        out_specs=both,
        check_vma=False,
    )
```

```python
import functools

import jax
import jax.numpy as jnp
from jax import lax
from jax.experimental import pallas as pl
from jax.experimental.pallas import tpu as pltpu
from jax.sharding import PartitionSpec as P

F32 = jnp.float32
BF = jnp.bfloat16
AXES = ("grp", "dev")
GROUPS = 16
DEVICES = 128
LEAVES = 16
STEPS = 128 // LEAVES


def dot(a, b):
    return jnp.dot(a, b, preferred_element_type=F32)


def dot_nt(a, b):
    return lax.dot_general(a, b, (((1,), (1,)), ((), ())), preferred_element_type=F32)


def iota(shape, dim):
    return lax.broadcasted_iota(jnp.int32, shape, dim)


def ones_where(condition):
    return jnp.where(condition, 1.0, 0.0).astype(BF)


def low_lanes(shape):
    return iota(shape, len(shape) - 1) < 64


def spread(half):
    shape = (64, 256)
    return ones_where(iota(shape, 0) == 2 * (iota(shape, 1) // 8) + half)


def gather_back(half):
    shape = (128, 256)
    return ones_where(iota(shape, 0) % 64 == 2 * (iota(shape, 1) // 8) + half)


def own_child():
    shape = (128, 256)
    return iota(shape, 0) // 16 == iota(shape, 1) % 8


def fold_halves(first, second):
    v = jnp.where(low_lanes(first.shape), first, second)
    return v + pltpu.roll(v, 64, 1)


def both_halves(v):
    low = low_lanes(v.shape)
    zero = jnp.zeros_like(v)
    return jnp.concatenate([jnp.where(low, v, zero), jnp.where(low, zero, v)], axis=0)


def up_pass(loads, points_ready, coefs_ready, pt, basis, tl, tm, xp, cp, mc, tops, xd, cd, own_at):
    e01 = jnp.concatenate([spread(0), spread(1)], axis=1)
    shape = (2048, 512)
    own = (iota(shape, 0) // 16) % 8 == iota(shape, 1) % 8
    shape = (128, 64)
    pick = ones_where(
        (iota(shape, 0) // 16 == iota(shape, 1) % 8)
        & ((iota(shape, 0) % 16) // 2 == iota(shape, 1) // 8)
    )
    shape = (128, 128)
    fold = ones_where(iota(shape, 0) % 64 == iota(shape, 1) % 64)
    parity = iota(shape, 1) // 64 == iota(shape, 0) % 2

    def expanded(v):
        n = v.shape[0]
        return jnp.where(own[:n], dot(v[:, :64], e01), 0.0)

    def parents(v, blocks):
        n = len(blocks)
        lhs = jnp.sum(expanded(v).reshape(n, 8, 16, 512), axis=1).astype(BF)
        out = []
        for k in range(n):
            d = dot(jnp.concatenate([lhs[k, :, :256], lhs[k, :, 256:]], axis=0), blocks[k])
            out.append(fold_halves(d[:16], d[16:]).astype(BF))
        return jnp.concatenate(out, axis=0)

    loads[0].wait()
    a = [jnp.where(parity, dot(pick, pt[k]), 0.0).astype(BF) for k in range(GROUPS)]
    x = dot(jnp.concatenate(a, axis=0), fold).astype(BF)
    low = low_lanes((1024, 128))
    xp[...] = jnp.where(low, x[:1024], x[1024:])
    points_ready()
    at = pl.ds(pl.multiple_of(own_at, 128), 128)
    xd[at] = x.reshape(128, 16, 128)
    wide = expanded(x).astype(BF)
    loads[1].wait()
    coef = []
    for k in range(GROUPS):
        w = wide[128 * k : 128 * (k + 1)]
        c = dot(jnp.concatenate([w[:, :256], w[:, 256:]], axis=0), basis[k])
        coef.append(fold_halves(c[:128], c[128:]).astype(BF))
    coef = jnp.concatenate(coef, axis=0)
    cp[...] = jnp.where(low, coef[:1024], coef[1024:])
    coefs_ready()
    cd[at] = coef.reshape(128, 16, 128)
    loads[2].wait()
    mc[...] = parents(coef, [tl[k] for k in range(GROUPS)])
    loads[3].wait()
    both = parents(mc[...], [tm[0], tm[1]])
    tops[...] = jnp.where(low_lanes((16, 128)), both[:16], both[16:])


def regroup():
    shape = (256, 256)
    row, col = iota(shape, 0), iota(shape, 1)
    return ones_where((row // 32 == col % 8) & (row % 32 == col // 8))


def widen(half):
    shape = (32, 128)
    return ones_where(iota(shape, 1) % 64 == 2 * iota(shape, 0) + half)


def blocks_times(sources, regrouped):
    lhs = jnp.concatenate(sources, axis=1)
    rhs = jnp.concatenate([regrouped[32 * j : 32 * (j + 1)] for j in range(8)], axis=1)
    return dot_nt(lhs, rhs)


def place_messages(cm, mt, mc, msgs, cb, formed):
    rep = iota((8, 8, 128), 2) // 32

    def mid_step(s, carry):
        y = both_halves(mc[pl.ds(pl.multiple_of(s * 16, 16), 16), :])
        y = jnp.concatenate([y] * 4, axis=0)
        zero = jnp.zeros_like(y)
        top = jnp.concatenate([y, zero], axis=1)
        low = jnp.concatenate([zero, y], axis=1)
        block = jnp.concatenate([cm[s, 0:256, :], cm[s, 256:512, :]], axis=1)
        r = dot_nt(block, jnp.concatenate([top, low], axis=0))
        parts = []
        for jh in range(2):
            b = r[:, 128 * jh : 128 * jh + 128].reshape(8, 4, 8, 128)
            q = b[:, 0]
            for k in range(1, 4):
                q = jnp.where(rep == k, b[:, k], q)
            parts.append(q)
        cb[:, pl.ds(pl.multiple_of(s * 16, 16), 16), :] = jnp.concatenate(parts, axis=1).astype(BF)
        return carry

    lax.fori_loop(0, GROUPS, mid_step, 0, unroll=4)

    target = mt[...]
    owner = target // 16
    parts = (owner // 32, (owner // 8) % 4, (owner // 2) % 4, owner % 2, target % 16)
    parts = jnp.concatenate(parts, axis=0).astype(F32).astype(BF)
    shape = (16, 256)
    along = ones_where(iota(shape, 1) % 16 == iota(shape, 0))
    mine = iota(shape, 1) // 16 == iota(shape, 0)
    parts = dot(parts, along)
    y, x, z, c, local = [
        jnp.sum(jnp.where(mine, parts[16 * k : 16 * k + 16], 0.0), axis=0, keepdims=True)
        for k in range(5)
    ]
    shape = (128, 256)
    onehot = iota(shape, 0).astype(F32) == 32.0 * y + 8.0 * x + 2.0 * z + c
    shape = (256, 256)
    earlier = ones_where(iota(shape, 0) < iota(shape, 1))
    rank = jnp.where(onehot, dot(ones_where(onehot), earlier), 0.0)
    rank = jnp.sum(rank, axis=0, keepdims=True)

    plans = (
        (0, 3, 2.0 * x + c, 4.0 * z + y),
        (3, 2, 2.0 * z + c, 4.0 * y + x),
        (5, 3, 2.0 * y + c, 4.0 * x + z),
    )
    for n, (first, count, stop, rest) in enumerate(plans):
        msg = msgs[n]
        at = 4.0 * rest + rank
        slot = iota((512, 256), 0).astype(F32)
        place = ones_where(slot == 64.0 * stop + at)
        wide = jnp.concatenate([cb[first + k] for k in range(count)], axis=1)
        wide = dot(place, wide).astype(BF)
        for k in range(count):
            rows = wide[:, 128 * k : 128 * k + 128].reshape(8, 64, 128)
            msg[:, 64 * k : 64 * k + 64, :] = rows
        shape = (128, 256)
        to_stop = (iota(shape, 0) // 16).astype(F32) == stop
        value = jnp.where(to_stop, local + 1.0, 0.0).astype(BF)
        lane = ones_where((iota(shape, 0) % 64).astype(F32) == at)
        label = dot_nt(value, lane) - 1.0
        msg[:, 64 * count : 64 * count + 16, :] = label.astype(BF).reshape(8, 16, 128)
        formed(n)


def sum_messages(count, landed, sums):
    shape = (16, 128)
    first = iota(shape, 1) < 64
    labels = pl.ds(64 * count, 16)
    lab = [
        jnp.where(first, landed[2 * q, labels, :], landed[2 * q + 1, labels, :])
        for q in range(4)
    ]
    lab = jnp.concatenate(lab, axis=1).astype(F32)
    shape = (16, 512)
    hit = lab == iota(shape, 0).astype(F32)
    to = (iota(shape, 1) // 4) % 16
    lhs = jnp.concatenate([ones_where(hit & (to == n)) for n in range(16)], axis=0)
    parts = [landed[:, 64 * k : 64 * k + 64, :].reshape(512, 128) for k in range(count)]
    total = dot(lhs, jnp.concatenate(parts, axis=1)).astype(BF)
    sums[...] = total.reshape(4, 64, 128 * count)


def near_kernel(
    near_idx, far_idx, ft, mt, near_in, far_in, pt_in, basis_in, tl_in, tm_in, cm_in, tc_in,
    out,
    near, far, near_sum, far_sum, near_part, far_part, down, xd, cd, stage, xland, cland, bw, cm, cb, pt, basis, tl, tm, tc, xp, cp, mc, tops,
    all_tops,
    msg_a, msg_b, msg_c, land_a, land_b, land_c,
    sum_a, sum_b, sum_c, next_a, next_b, next_c, part_a, part_b, part_c,
    sums_a, sums_b, sums_c, send, recv, here, fetch,
):
    y = lax.axis_index("grp")
    dev = lax.axis_index("dev")
    x, z, c = dev // 8, (dev // 2) % 4, dev % 2
    me = y * 32 + dev
    right = lax.rem(me + 1, DEVICES)
    left = lax.rem(me + DEVICES - 1, DEVICES)
    mesh = pl.DeviceIdType.MESH

    def remote(src, dst, n, device):
        return pltpu.make_async_remote_copy(
            src_ref=src,
            dst_ref=dst,
            send_sem=send.at[n],
            recv_sem=recv.at[n],
            device_id=device,
            device_id_type=mesh,
        )

    def at_x(k):
        return (y, lax.rem(x + k, 4) * 8 + z * 2 + c)

    def at_y(k):
        return (lax.rem(y + k, 4), dev)

    def at_z(k):
        return (y, x * 8 + lax.rem(z + k, 4) * 2 + c)

    def at_xc(k):
        m = lax.rem(x * 2 + c + k, 8)
        return (y, (m // 2) * 8 + z * 2 + m % 2)

    def at_yc(k):
        m = lax.rem(y * 2 + c + k, 8)
        return (m // 2, x * 8 + z * 2 + m % 2)

    def at_zc(k):
        return (y, x * 8 + lax.rem(z * 2 + c + k, 8))

    def halos(n):
        src, dst = ((xp, xland), (cp, cland))[n]
        return [
            remote(src, dst.at[k], 2 * n + k, (to // 32, to % 32))
            for k, to in enumerate((right, left))
        ]

    def tops_to(n):
        if n == 0:
            return [remote(tops, all_tops.at[c, y, z, x], 3 + k, at_x(k)) for k in range(1, 4)]
        if n == 1:
            block = all_tops.at[c, y, z]
            return [remote(block, block, 6 + k, at_z(k)) for k in range(1, 4)]
        if n == 2:
            block = all_tops.at[c, y]
            return [remote(block, block, 9 + k, at_y(k)) for k in range(1, 4)]
        block = all_tops.at[c]
        return [remote(block, block, 13, (y, x * 8 + z * 2 + 1 - c))]

    plans = (
        (3, (x, z, y), (at_xc, at_z, at_y), msg_a, land_a, sum_a, next_a, part_a, sums_a),
        (2, (z, y, x), (at_zc, at_y, at_x), msg_b, land_b, sum_b, next_b, part_b, sums_b),
        (3, (y, x, z), (at_yc, at_x, at_z), msg_c, land_c, sum_c, next_c, part_c, sums_c),
    )

    def first_hop(n):
        _, (a, _, _), (to, _, _), msg, land = plans[n][:5]
        own = a * 2 + c
        return [
            remote(msg.at[lax.rem(own + k, 8)], land.at[own], 13 + 7 * n + k, to(k))
            for k in range(1, 8)
        ]

    def second_hop(n):
        _, (_, a, _), (_, to, _), _, _, src, dst = plans[n][:7]
        return [
            remote(src.at[lax.rem(a + k, 4)], dst.at[a], 34 + 3 * n + k, to(k))
            for k in range(1, 4)
        ]

    def third_hop(n):
        _, (_, _, a), (_, _, to), _, _, _, _, src, dst = plans[n]
        return [
            remote(src.at[lax.rem(a + k, 4)], dst.at[a], 43 + 3 * n + k, to(k))
            for k in range(1, 4)
        ]

    def own_first(n):
        own = plans[n][1][0] * 2 + c
        return pltpu.make_async_copy(plans[n][3].at[own], plans[n][4].at[own], here.at[n])

    def own_third(n):
        own = plans[n][1][2]
        return pltpu.make_async_copy(plans[n][7].at[own], plans[n][8].at[own], here.at[3 + n])

    def own_tops():
        return pltpu.make_async_copy(tops, all_tops.at[c, y, z, x], here.at[6])

    def chunk(src, dst, base, n):
        part = pl.ds(n * LEAVES, LEAVES)
        return pltpu.make_async_copy(src.at[part], dst.at[part], fetch.at[base + n])

    def start(copies):
        for copy in copies:
            copy.start()

    def arrive(copies):
        for copy in copies:
            copy.wait_recv()

    low = low_lanes((1024, 128))

    def unpack(dst, part, n):
        shape = (128, 128)
        swap = ones_where((iota(shape, 0) + 64) % 128 == iota(shape, 1))
        v = part[...]
        w = dot(v, swap).astype(BF)
        for h, (lo, hi) in enumerate(((v, w), (w, v))):
            at = pl.ds(pl.multiple_of((dev + n) % 4 * 128 + h * 64, 64), 64)
            dst[at] = jnp.where(low, lo, hi).reshape(64, 16, 128)

    pairs = (
        (pt_in, pt), (basis_in, basis), (tl_in, tl), (tm_in, tm), (cm_in, cm), (tc_in, tc),
    )
    loads = [
        pltpu.make_async_copy(src, dst, here.at[7 + n]) for n, (src, dst) in enumerate(pairs)
    ]
    start(loads)
    barrier = pltpu.get_barrier_semaphore()

    def greet(device):
        pl.semaphore_signal(barrier, inc=1, device_id=device, device_id_type=mesh)

    for to in (right, left):
        greet((to // 32, to % 32))
    for k in range(1, 8):
        greet(at_xc(k))
        greet(at_yc(k))
        greet(at_zc(k))

    def points_ready():
        pl.semaphore_wait(barrier, 23)
        start(halos(0))
        start([chunk(near_in, near, 0, n) for n in range(STEPS)])

    def coefs_ready():
        start(halos(1))
        start([chunk(far_in, far, STEPS, n) for n in range(STEPS)])

    up_pass(loads, points_ready, coefs_ready, pt, basis, tl, tm, xp, cp, mc, tops, xd, cd, dev % 4 * 128)
    start(tops_to(0))
    own_tops().start()
    loads[4].wait()
    loads[5].wait()

    def formed(n):
        start(first_hop(n))
        own_first(n).start()

    place_messages(cm, mt, mc, (msg_a, msg_b, msg_c), cb, formed)
    bw[0] = gather_back(0)
    bw[1] = gather_back(1)
    arrive(halos(0))
    unpack(xd, xland.at[0], 3)
    unpack(xd, xland.at[1], 1)

    def work(g, idx, blocks, src, out):
        low_f = low_lanes((32, 128))
        low_x = low_lanes((16, 128))
        for i in range(LEAVES):
            at = g * LEAVES + i
            plane = stage.at[i]
            plane[...] = blocks[at].astype(F32)
            found = [src[idx[j, at] & 511] for j in range(8)]
            lhs, first, second = [], [], []
            for j in range(0, 8, 2):
                lhs.append(jnp.where(low_x, found[j], found[j + 1]))
                even = plane[pl.ds(j, 32, stride=8), :]
                odd = plane[pl.ds(j + 1, 32, stride=8), :]
                turned = pltpu.roll(jnp.where(low_f, odd, even), 64, 1)
                first.append(jnp.where(low_f, even, turned).astype(BF))
                second.append(jnp.where(low_f, turned, odd).astype(BF))
            rhs = [jnp.concatenate(v, axis=1) for v in (first, second)]
            o = dot_nt(jnp.concatenate(lhs, axis=1), jnp.concatenate(rhs, axis=0))
            rows = pl.ds(pl.multiple_of(at * 16, 16), 16)
            out[rows, :] = o

    def near_step(g, carry):
        @pl.when(g == 1)
        def _():
            own_tops().wait()
            arrive(tops_to(0))
            start(tops_to(1))

        @pl.when(g == 3)
        def _():
            arrive(tops_to(1))
            start(tops_to(2))

        @pl.when(g == STEPS - 1)
        def _():
            arrive(tops_to(2))
            start(tops_to(3))

        chunk(near_in, near, 0, g).wait()
        work(g, near_idx, near, xd, near_sum)
        return carry

    lax.fori_loop(0, STEPS, near_step, 0)
    arrive(halos(1))
    unpack(cd, cland.at[0], 3)
    unpack(cd, cland.at[1], 1)

    def far_step(g, carry):
        @pl.when(g == 2)
        def _():
            for n in range(3):
                own_first(n).wait()
                arrive(first_hop(n))
            for n in range(3):
                sum_messages(plans[n][0], plans[n][4], plans[n][5])
            for n in range(3):
                start(second_hop(n))

        @pl.when(g == STEPS - 1)
        def _():
            for n in range(3):
                arrive(second_hop(n))
            for n in range(3):
                at, own, got, dst = plans[n][1][1], plans[n][5], plans[n][6], plans[n][7]
                total = own[at].astype(F32)
                for k in range(1, 4):
                    total = total + got[lax.rem(at + k, 4)].astype(F32)
                dst[...] = total.astype(BF).reshape(dst.shape)
            for n in range(3):
                start(third_hop(n))
                own_third(n).start()

        chunk(far_in, far, STEPS, g).wait()
        work(g, far_idx, far, cd, far_sum)
        return carry

    lax.fori_loop(0, STEPS, far_step, 0)
    arrive(tops_to(3))
    b0, b1 = bw[0], bw[1]
    down[...] = from_tops(ft, all_tops, tc, tm, b0, b1)
    shape = (64, 128)
    row = iota(shape, 0)
    in_order = ones_where(iota(shape, 1) % 64 == 2 * (row % 32) + row // 32)
    near_part[...] = dot(near_sum[...].astype(BF), in_order)
    far_part[...] = dot(far_sum[...].astype(BF), in_order)
    for n in range(3):
        own_third(n).wait()
        arrive(third_hop(n))
    fields = (from_mids((sums_a, sums_b, sums_c)) + down[...]).astype(BF)
    leaves_out(fields, tl, basis, near_part[...], far_part[...], b0, b1, out)
    sent = [halos(0), halos(1)] + [tops_to(n) for n in range(4)]
    for n in range(3):
        sent += [first_hop(n), second_hop(n), third_hop(n)]
    for copies in sent:
        for copy in copies:
            copy.wait_send()


def converted(first, second, b0, b1):
    first = jnp.concatenate(first, axis=0)
    second = jnp.concatenate(second, axis=0)
    return dot_nt(first, b0) + dot_nt(second, b1)


def for_children(field, t):
    own = own_child()
    d = dot_nt(both_halves(field), t)
    return [
        jnp.where(own, jnp.concatenate([d[16 * k : 16 * k + 16]] * 8, axis=0), 0.0)
        for k in range(2)
    ]


def from_tops(ft, all_tops, tc, tm, b0, b1):
    w0, w1 = widen(0), widen(1)
    order = regroup()
    shape = (128, 128)
    fold = ones_where(iota(shape, 0) % 64 == iota(shape, 1) % 64)
    shape = (16, 128)
    half = iota(shape, 1) // 64
    found = []
    for n in range(32):
        top = ft[n // 16, n % 16]
        dev = top // 2
        y, x, z, c = dev // 32, (dev // 8) % 4, (dev // 2) % 4, dev % 2
        v = all_tops[c, y, z, x]
        found.append(jnp.where(half == top % 2, v, jnp.zeros_like(v)))
    found = dot(jnp.concatenate(found, axis=0), fold).astype(BF)
    fields = []
    for t in range(2):
        total = jnp.zeros((32, 32), F32)
        for jh in range(2):
            regrouped = dot(order, tc[t, jh * 256 : (jh + 1) * 256, :]).astype(BF)
            first = (t * 16 + jh * 8) * 16
            srcs = [both_halves(found[first + 16 * j : first + 16 * (j + 1)]) for j in range(8)]
            total = total + blocks_times(srcs, regrouped)
        total = total.astype(BF)
        fields.append((dot(total[:16], w0) + dot(total[16:], w1)).astype(BF))
    first, second = zip(*[for_children(fields[t], tm[t]) for t in range(2)])
    return converted([v.astype(BF) for v in first], [v.astype(BF) for v in second], b0, b1)


def from_mids(parts):
    wide = []
    for part in parts:
        total = part[0].astype(F32)
        for k in range(1, 4):
            total = total + part[k].astype(F32)
        wide.append(total)
    wide = jnp.concatenate(wide, axis=1).astype(BF)
    shape = (256, 16)
    repeat = ones_where(iota(shape, 0) // 16 == iota(shape, 1))
    shape = (256, 1024)
    keep = iota(shape, 1) % 16 == iota(shape, 0) % 16
    m = jnp.where(keep, dot(repeat, wide), 0.0).astype(BF)
    shape = (1024, 128)
    to_m = ones_where(iota(shape, 0) // 16 == iota(shape, 1) % 64)
    return dot(m, to_m)


def leaves_out(fields, tl, basis, near_part, far_part, b0, b1, out):
    own = own_child()
    shape = (64, 128)
    row, col = iota(shape, 0), iota(shape, 1)
    same = row % 8 == col // 16
    pick0 = ones_where(same & (col % 16 == 2 * (row // 8)))
    pick1 = ones_where(same & (col % 16 == 2 * (row // 8) + 1))
    low = low_lanes(shape)
    first, second = [], []
    for k in range(GROUPS):
        m0, m1 = for_children(fields[16 * k : 16 * k + 16], tl[k])
        first.append(m0.astype(BF))
        second.append(m1.astype(BF))
    leaf = (converted(first, second, b0, b1) + far_part).astype(BF)
    first, second = [], []
    for k in range(GROUPS):
        z = dot_nt(both_halves(leaf[128 * k : 128 * k + 128]), basis[k])
        first.append(jnp.where(own, z[:128], 0.0).astype(BF))
        second.append(jnp.where(own, z[128:], 0.0).astype(BF))
    total = (converted(first, second, b0, b1) + near_part).astype(BF)
    for k in range(GROUPS):
        v = total[128 * k : 128 * (k + 1)]
        out[k] = jnp.where(low, dot(pick0, v), dot(pick1, v)).astype(BF)


def as_tiles(a):
    n = a.shape[0]
    return a.reshape(n, 8, 32, 128).transpose(0, 2, 1, 3).reshape(n, 256, 128)


VMEM = pl.BlockSpec(memory_space=pltpu.VMEM)
ANY = pl.BlockSpec(memory_space=pl.ANY)
SMEM = pl.BlockSpec(memory_space=pltpu.SMEM)
LIMIT = 56 * 1024 * 1024


def body(
    points,
    basis,
    transfer_leaf,
    transfer_mid,
    near_blocks,
    near_src,
    leaf_coupling,
    far_leaf,
    mid_coupling,
    mid_target,
    top_coupling,
    far_top,
):
    pt = points.reshape(16, 8, 8, 128).transpose(0, 2, 1, 3).reshape(16, 64, 128)
    bt = as_tiles(basis.reshape(16, 8, 4096))
    tl = as_tiles(transfer_leaf.reshape(16, 8, 4096))
    tm = as_tiles(transfer_mid.reshape(2, 8, 4096))
    cm = as_tiles(mid_coupling.reshape(32, 8, 4096)).reshape(16, 512, 128)
    tc = as_tiles(top_coupling.reshape(4, 8, 4096)).reshape(2, 512, 128)
    nb = as_tiles(near_blocks)
    fb = as_tiles(leaf_coupling)

    lanes = (384, 256, 384)
    out = pl.pallas_call(
        near_kernel,
        out_shape=jax.ShapeDtypeStruct((16, 64, 128), BF),
        in_specs=[SMEM] * 3 + [VMEM] + [ANY] * 8,
        out_specs=VMEM,
        scratch_shapes=[
            pltpu.VMEM((128, 256, 128), BF),
            pltpu.VMEM((128, 256, 128), BF),
            pltpu.VMEM((2048, 64), F32),
            pltpu.VMEM((2048, 64), F32),
            pltpu.VMEM((2048, 128), F32),
            pltpu.VMEM((2048, 128), F32),
            pltpu.VMEM((256, 128), F32),
            pltpu.VMEM((512, 16, 128), BF),
            pltpu.VMEM((512, 16, 128), BF),
            pltpu.VMEM((LEAVES, 256, 128), F32),
            pltpu.VMEM((2, 1024, 128), BF),
            pltpu.VMEM((2, 1024, 128), BF),
            pltpu.VMEM((2, 128, 256), BF),
            pltpu.VMEM((16, 512, 128), BF),
            pltpu.VMEM((8, 256, 128), BF),
            pltpu.VMEM((16, 64, 128), BF),
            pltpu.VMEM((16, 256, 128), BF),
            pltpu.VMEM((16, 256, 128), BF),
            pltpu.VMEM((2, 256, 128), BF),
            pltpu.VMEM((2, 512, 128), BF),
            pltpu.VMEM((1024, 128), BF),
            pltpu.VMEM((1024, 128), BF),
            pltpu.VMEM((256, 128), BF),
            pltpu.VMEM((16, 128), BF),
            pltpu.VMEM((2, 4, 4, 4, 16, 128), BF),
        ]
        + [pltpu.VMEM((8, n // 2 + 16, 128), BF) for n in lanes] * 2
        + [pltpu.VMEM((4, 64, n), BF) for n in lanes] * 2
        + [pltpu.VMEM((4, 16, n), BF) for n in lanes] * 2
        + [
            pltpu.SemaphoreType.DMA((53,)),
            pltpu.SemaphoreType.DMA((53,)),
            pltpu.SemaphoreType.DMA((13,)),
            pltpu.SemaphoreType.DMA((2 * STEPS,)),
        ],
        compiler_params=pltpu.CompilerParams(
            vmem_limit_bytes=LIMIT, collective_id=0, has_side_effects=True
        ),
        name="whole",
    )(near_src.T, far_leaf.T, far_top, mid_target, nb, fb, pt, bt, tl, tm, cm, tc)
    return out.reshape(16, 8, 8, 128).transpose(0, 2, 1, 3).reshape(128, 1024)


def solution(mesh):
    both = P(AXES, None)
    three = P(AXES, None, None)
    return jax.shard_map(
        body,
        mesh=mesh,
        in_specs=(
            both, both, both, both, three, both, three, both, three, both, three, both,
        ),
        out_specs=both,
        check_vma=False,
    )
```

```python
import functools

import jax
import jax.numpy as jnp
from jax import lax
from jax.experimental import pallas as pl
from jax.experimental.pallas import tpu as pltpu
from jax.sharding import PartitionSpec as P

F32 = jnp.float32
BF = jnp.bfloat16
AXES = ("grp", "dev")
GROUPS = 16
DEVICES = 128
LEAVES = 16
STEPS = 128 // LEAVES


def dot(a, b):
    return jnp.dot(a, b, preferred_element_type=F32)


def dot_nt(a, b):
    return lax.dot_general(a, b, (((1,), (1,)), ((), ())), preferred_element_type=F32)


def iota(shape, dim):
    return lax.broadcasted_iota(jnp.int32, shape, dim)


def ones_where(condition):
    return jnp.where(condition, 1.0, 0.0).astype(BF)


def low_lanes(shape):
    return iota(shape, len(shape) - 1) < 64


def spread(half):
    shape = (64, 256)
    return ones_where(iota(shape, 0) == 2 * (iota(shape, 1) // 8) + half)


def gather_back(half):
    shape = (128, 256)
    return ones_where(iota(shape, 0) % 64 == 2 * (iota(shape, 1) // 8) + half)


def own_child():
    shape = (128, 256)
    return iota(shape, 0) // 16 == iota(shape, 1) % 8


def fold_halves(first, second):
    v = jnp.where(low_lanes(first.shape), first, second)
    return v + pltpu.roll(v, 64, 1)


def both_halves(v):
    low = low_lanes(v.shape)
    zero = jnp.zeros_like(v)
    return jnp.concatenate([jnp.where(low, v, zero), jnp.where(low, zero, v)], axis=0)


def up_pass(loads, points_ready, coefs_ready, pt, basis, tl, tm, xp, cp, mc, tops, xd, cd, own_at):
    e01 = jnp.concatenate([spread(0), spread(1)], axis=1)
    shape = (2048, 512)
    own = (iota(shape, 0) // 16) % 8 == iota(shape, 1) % 8
    shape = (128, 64)
    pick = ones_where(
        (iota(shape, 0) // 16 == iota(shape, 1) % 8)
        & ((iota(shape, 0) % 16) // 2 == iota(shape, 1) // 8)
    )
    shape = (128, 128)
    fold = ones_where(iota(shape, 0) % 64 == iota(shape, 1) % 64)
    parity = iota(shape, 1) // 64 == iota(shape, 0) % 2

    def expanded(v):
        n = v.shape[0]
        return jnp.where(own[:n], dot(v[:, :64], e01), 0.0)

    def parents(v, blocks):
        n = len(blocks)
        lhs = jnp.sum(expanded(v).reshape(n, 8, 16, 512), axis=1).astype(BF)
        out = []
        for k in range(n):
            d = dot(jnp.concatenate([lhs[k, :, :256], lhs[k, :, 256:]], axis=0), blocks[k])
            out.append(fold_halves(d[:16], d[16:]).astype(BF))
        return jnp.concatenate(out, axis=0)

    loads[0].wait()
    a = [jnp.where(parity, dot(pick, pt[k]), 0.0).astype(BF) for k in range(GROUPS)]
    x = dot(jnp.concatenate(a, axis=0), fold).astype(BF)
    low = low_lanes((1024, 128))
    xp[...] = jnp.where(low, x[:1024], x[1024:])
    points_ready()
    at = pl.ds(pl.multiple_of(own_at, 128), 128)
    xd[at] = x.reshape(128, 16, 128)
    wide = expanded(x).astype(BF)
    loads[1].wait()
    coef = []
    for k in range(GROUPS):
        w = wide[128 * k : 128 * (k + 1)]
        c = dot(jnp.concatenate([w[:, :256], w[:, 256:]], axis=0), basis[k])
        coef.append(fold_halves(c[:128], c[128:]).astype(BF))
    coef = jnp.concatenate(coef, axis=0)
    cp[...] = jnp.where(low, coef[:1024], coef[1024:])
    coefs_ready()
    cd[at] = coef.reshape(128, 16, 128)
    loads[2].wait()
    mc[...] = parents(coef, [tl[k] for k in range(GROUPS)])
    loads[3].wait()
    both = parents(mc[...], [tm[0], tm[1]])
    tops[...] = jnp.where(low_lanes((16, 128)), both[:16], both[16:])


def regroup():
    shape = (256, 256)
    row, col = iota(shape, 0), iota(shape, 1)
    return ones_where((row // 32 == col % 8) & (row % 32 == col // 8))


def widen(half):
    shape = (32, 128)
    return ones_where(iota(shape, 1) % 64 == 2 * iota(shape, 0) + half)


def blocks_times(sources, regrouped):
    lhs = jnp.concatenate(sources, axis=1)
    rhs = jnp.concatenate([regrouped[32 * j : 32 * (j + 1)] for j in range(8)], axis=1)
    return dot_nt(lhs, rhs)


def place_messages(cm, mt, mc, msgs, cb, formed):
    rep = iota((8, 8, 128), 2) // 32

    def mid_step(s, carry):
        y = both_halves(mc[pl.ds(pl.multiple_of(s * 16, 16), 16), :])
        y = jnp.concatenate([y] * 4, axis=0)
        zero = jnp.zeros_like(y)
        top = jnp.concatenate([y, zero], axis=1)
        low = jnp.concatenate([zero, y], axis=1)
        block = jnp.concatenate([cm[s, 0:256, :], cm[s, 256:512, :]], axis=1)
        r = dot_nt(block, jnp.concatenate([top, low], axis=0))
        parts = []
        for jh in range(2):
            b = r[:, 128 * jh : 128 * jh + 128].reshape(8, 4, 8, 128)
            q = b[:, 0]
            for k in range(1, 4):
                q = jnp.where(rep == k, b[:, k], q)
            parts.append(q)
        cb[:, pl.ds(pl.multiple_of(s * 16, 16), 16), :] = jnp.concatenate(parts, axis=1).astype(BF)
        return carry

    lax.fori_loop(0, GROUPS, mid_step, 0, unroll=4)

    target = mt[...]
    owner = target // 16
    parts = (owner // 32, (owner // 8) % 4, (owner // 2) % 4, owner % 2, target % 16)
    parts = jnp.concatenate(parts, axis=0).astype(F32).astype(BF)
    shape = (16, 256)
    along = ones_where(iota(shape, 1) % 16 == iota(shape, 0))
    mine = iota(shape, 1) // 16 == iota(shape, 0)
    parts = dot(parts, along)
    y, x, z, c, local = [
        jnp.sum(jnp.where(mine, parts[16 * k : 16 * k + 16], 0.0), axis=0, keepdims=True)
        for k in range(5)
    ]
    shape = (128, 256)
    onehot = iota(shape, 0).astype(F32) == 32.0 * y + 8.0 * x + 2.0 * z + c
    shape = (256, 256)
    earlier = ones_where(iota(shape, 0) < iota(shape, 1))
    rank = jnp.where(onehot, dot(ones_where(onehot), earlier), 0.0)
    rank = jnp.sum(rank, axis=0, keepdims=True)

    plans = (
        (0, 3, 2.0 * x + c, 4.0 * z + y),
        (3, 2, 2.0 * z + c, 4.0 * y + x),
        (5, 3, 2.0 * y + c, 4.0 * x + z),
    )
    for n, (first, count, stop, rest) in enumerate(plans):
        msg = msgs[n]
        at = 4.0 * rest + rank
        slot = iota((512, 256), 0).astype(F32)
        place = ones_where(slot == 64.0 * stop + at)
        wide = jnp.concatenate([cb[first + k] for k in range(count)], axis=1)
        wide = dot(place, wide).astype(BF)
        for k in range(count):
            rows = wide[:, 128 * k : 128 * k + 128].reshape(8, 64, 128)
            msg[:, 64 * k : 64 * k + 64, :] = rows
        shape = (128, 256)
        to_stop = (iota(shape, 0) // 16).astype(F32) == stop
        value = jnp.where(to_stop, local + 1.0, 0.0).astype(BF)
        lane = ones_where((iota(shape, 0) % 64).astype(F32) == at)
        label = dot_nt(value, lane) - 1.0
        msg[:, 64 * count : 64 * count + 16, :] = label.astype(BF).reshape(8, 16, 128)
        formed(n)


def sum_messages(count, landed, sums):
    shape = (16, 128)
    first = iota(shape, 1) < 64
    labels = pl.ds(64 * count, 16)
    lab = [
        jnp.where(first, landed[2 * q, labels, :], landed[2 * q + 1, labels, :])
        for q in range(4)
    ]
    lab = jnp.concatenate(lab, axis=1).astype(F32)
    shape = (16, 512)
    hit = lab == iota(shape, 0).astype(F32)
    to = (iota(shape, 1) // 4) % 16
    lhs = jnp.concatenate([ones_where(hit & (to == n)) for n in range(16)], axis=0)
    parts = [landed[:, 64 * k : 64 * k + 64, :].reshape(512, 128) for k in range(count)]
    total = dot(lhs, jnp.concatenate(parts, axis=1)).astype(BF)
    sums[...] = total.reshape(4, 64, 128 * count)


def near_kernel(
    near_idx, far_idx, ft, mt, near_in, far_in, pt_in, basis_in, tl_in, tm_in, cm_in, tc_in,
    out,
    near, far, near_sum, far_sum, near_part, far_part, down, xd, cd, stage, xland, cland, bw, cm, cb, pt, basis, tl, tm, tc, xp, cp, mc, tops,
    all_tops,
    msg_a, msg_b, msg_c, land_a, land_b, land_c,
    sum_a, sum_b, sum_c, next_a, next_b, next_c, part_a, part_b, part_c,
    sums_a, sums_b, sums_c, send, recv, here, fetch,
):
    y = lax.axis_index("grp")
    dev = lax.axis_index("dev")
    x, z, c = dev // 8, (dev // 2) % 4, dev % 2
    me = y * 32 + dev
    right = lax.rem(me + 1, DEVICES)
    left = lax.rem(me + DEVICES - 1, DEVICES)
    mesh = pl.DeviceIdType.MESH

    def remote(src, dst, n, device):
        return pltpu.make_async_remote_copy(
            src_ref=src,
            dst_ref=dst,
            send_sem=send.at[n],
            recv_sem=recv.at[n],
            device_id=device,
            device_id_type=mesh,
        )

    def at_x(k):
        return (y, lax.rem(x + k, 4) * 8 + z * 2 + c)

    def at_y(k):
        return (lax.rem(y + k, 4), dev)

    def at_z(k):
        return (y, x * 8 + lax.rem(z + k, 4) * 2 + c)

    def at_xc(k):
        m = lax.rem(x * 2 + c + k, 8)
        return (y, (m // 2) * 8 + z * 2 + m % 2)

    def at_yc(k):
        m = lax.rem(y * 2 + c + k, 8)
        return (m // 2, x * 8 + z * 2 + m % 2)

    def at_zc(k):
        return (y, x * 8 + lax.rem(z * 2 + c + k, 8))

    def halos(n):
        src, dst = ((xp, xland), (cp, cland))[n]
        return [
            remote(src, dst.at[k], 2 * n + k, (to // 32, to % 32))
            for k, to in enumerate((right, left))
        ]

    def tops_to(n):
        if n == 0:
            return [remote(tops, all_tops.at[c, y, z, x], 3 + k, at_x(k)) for k in range(1, 4)]
        if n == 1:
            block = all_tops.at[c, y, z]
            return [remote(block, block, 6 + k, at_z(k)) for k in range(1, 4)]
        if n == 2:
            block = all_tops.at[c, y]
            return [remote(block, block, 9 + k, at_y(k)) for k in range(1, 4)]
        block = all_tops.at[c]
        return [remote(block, block, 13, (y, x * 8 + z * 2 + 1 - c))]

    plans = (
        (3, (x, z, y), (at_xc, at_z, at_y), msg_a, land_a, sum_a, next_a, part_a, sums_a),
        (2, (z, y, x), (at_zc, at_y, at_x), msg_b, land_b, sum_b, next_b, part_b, sums_b),
        (3, (y, x, z), (at_yc, at_x, at_z), msg_c, land_c, sum_c, next_c, part_c, sums_c),
    )

    def first_hop(n):
        _, (a, _, _), (to, _, _), msg, land = plans[n][:5]
        own = a * 2 + c
        return [
            remote(msg.at[lax.rem(own + k, 8)], land.at[own], 13 + 7 * n + k, to(k))
            for k in range(1, 8)
        ]

    def second_hop(n):
        _, (_, a, _), (_, to, _), _, _, src, dst = plans[n][:7]
        return [
            remote(src.at[lax.rem(a + k, 4)], dst.at[a], 34 + 3 * n + k, to(k))
            for k in range(1, 4)
        ]

    def third_hop(n):
        _, (_, _, a), (_, _, to), _, _, _, _, src, dst = plans[n]
        return [
            remote(src.at[lax.rem(a + k, 4)], dst.at[a], 43 + 3 * n + k, to(k))
            for k in range(1, 4)
        ]

    def own_first(n):
        own = plans[n][1][0] * 2 + c
        return pltpu.make_async_copy(plans[n][3].at[own], plans[n][4].at[own], here.at[n])

    def own_third(n):
        own = plans[n][1][2]
        return pltpu.make_async_copy(plans[n][7].at[own], plans[n][8].at[own], here.at[3 + n])

    def own_tops():
        return pltpu.make_async_copy(tops, all_tops.at[c, y, z, x], here.at[6])

    def chunk(src, dst, base, n):
        part = pl.ds(n * LEAVES, LEAVES)
        return pltpu.make_async_copy(src.at[part], dst.at[part], fetch.at[base + n])

    def start(copies):
        for copy in copies:
            copy.start()

    def arrive(copies):
        for copy in copies:
            copy.wait_recv()

    low = low_lanes((1024, 128))

    def unpack(dst, part, n):
        shape = (128, 128)
        swap = ones_where((iota(shape, 0) + 64) % 128 == iota(shape, 1))
        v = part[...]
        w = dot(v, swap).astype(BF)
        for h, (lo, hi) in enumerate(((v, w), (w, v))):
            at = pl.ds(pl.multiple_of((dev + n) % 4 * 128 + h * 64, 64), 64)
            dst[at] = jnp.where(low, lo, hi).reshape(64, 16, 128)

    pairs = (
        (pt_in, pt), (basis_in, basis), (tl_in, tl), (tm_in, tm), (cm_in, cm), (tc_in, tc),
    )
    loads = [
        pltpu.make_async_copy(src, dst, here.at[7 + n]) for n, (src, dst) in enumerate(pairs)
    ]
    start(loads)
    barrier = pltpu.get_barrier_semaphore()

    def greet(device):
        pl.semaphore_signal(barrier, inc=1, device_id=device, device_id_type=mesh)

    for to in (right, left):
        greet((to // 32, to % 32))
    for k in range(1, 8):
        greet(at_xc(k))
        greet(at_yc(k))
        greet(at_zc(k))

    def points_ready():
        pl.semaphore_wait(barrier, 23)
        start(halos(0))
        start([chunk(near_in, near, 0, n) for n in range(STEPS)])

    def coefs_ready():
        start(halos(1))
        start([chunk(far_in, far, STEPS, n) for n in range(STEPS)])

    up_pass(loads, points_ready, coefs_ready, pt, basis, tl, tm, xp, cp, mc, tops, xd, cd, dev % 4 * 128)
    start(tops_to(0))
    own_tops().start()
    loads[4].wait()
    loads[5].wait()

    def formed(n):
        start(first_hop(n))
        own_first(n).start()

    place_messages(cm, mt, mc, (msg_a, msg_b, msg_c), cb, formed)
    bw[0] = gather_back(0)
    bw[1] = gather_back(1)
    arrive(halos(0))
    unpack(xd, xland.at[0], 3)
    unpack(xd, xland.at[1], 1)

    def work(g, idx, blocks, src, out):
        low_f = low_lanes((32, 128))
        low_x = low_lanes((16, 128))
        for i in range(LEAVES):
            at = g * LEAVES + i
            plane = stage.at[i]
            plane[...] = blocks[at].astype(F32)
            found = [src[idx[j, at] & 511] for j in range(8)]
            lhs, first, second = [], [], []
            for j in range(0, 8, 2):
                lhs.append(jnp.where(low_x, found[j], found[j + 1]))
                even = plane[pl.ds(j, 32, stride=8), :]
                odd = plane[pl.ds(j + 1, 32, stride=8), :]
                turned = pltpu.roll(jnp.where(low_f, odd, even), 64, 1)
                first.append(jnp.where(low_f, even, turned).astype(BF))
                second.append(jnp.where(low_f, turned, odd).astype(BF))
            rhs = [jnp.concatenate(v, axis=1) for v in (first, second)]
            o = dot_nt(jnp.concatenate(lhs, axis=1), jnp.concatenate(rhs, axis=0))
            rows = pl.ds(pl.multiple_of(at * 16, 16), 16)
            out[rows, :] = o

    def near_step(g, carry):
        @pl.when(g == 1)
        def _():
            own_tops().wait()
            arrive(tops_to(0))
            start(tops_to(1))

        @pl.when(g == 3)
        def _():
            arrive(tops_to(1))
            start(tops_to(2))

        @pl.when(g == STEPS - 1)
        def _():
            arrive(tops_to(2))
            start(tops_to(3))

        chunk(near_in, near, 0, g).wait()
        work(g, near_idx, near, xd, near_sum)
        return carry

    lax.fori_loop(0, STEPS, near_step, 0)
    b0, b1 = bw[0], bw[1]
    shape = (64, 128)
    row = iota(shape, 0)
    in_order = ones_where(iota(shape, 1) % 64 == 2 * (row % 32) + row // 32)
    for n in range(3):
        own_first(n).wait()
        arrive(first_hop(n))
    for n in range(3):
        sum_messages(plans[n][0], plans[n][4], plans[n][5])
    for n in range(3):
        start(second_hop(n))
    arrive(tops_to(3))
    down[...] = from_tops(ft, all_tops, tc, tm, b0, b1)
    near_part[...] = dot(near_sum[...].astype(BF), in_order)
    arrive(halos(1))
    unpack(cd, cland.at[0], 3)
    unpack(cd, cland.at[1], 1)

    def far_step(g, carry):
        @pl.when(g == 5)
        def _():
            for n in range(3):
                arrive(second_hop(n))
            for n in range(3):
                at, own, got, dst = plans[n][1][1], plans[n][5], plans[n][6], plans[n][7]
                total = own[at].astype(F32)
                for k in range(1, 4):
                    total = total + got[lax.rem(at + k, 4)].astype(F32)
                dst[...] = total.astype(BF).reshape(dst.shape)
            for n in range(3):
                start(third_hop(n))
                own_third(n).start()

        chunk(far_in, far, STEPS, g).wait()
        work(g, far_idx, far, cd, far_sum)
        return carry

    lax.fori_loop(0, STEPS, far_step, 0)
    far_part[...] = dot(far_sum[...].astype(BF), in_order)
    for n in range(3):
        own_third(n).wait()
        arrive(third_hop(n))
    fields = (from_mids((sums_a, sums_b, sums_c)) + down[...]).astype(BF)
    leaves_out(fields, tl, basis, near_part[...], far_part[...], b0, b1, out)
    sent = [halos(0), halos(1)] + [tops_to(n) for n in range(4)]
    for n in range(3):
        sent += [first_hop(n), second_hop(n), third_hop(n)]
    for copies in sent:
        for copy in copies:
            copy.wait_send()


def converted(first, second, b0, b1):
    first = jnp.concatenate(first, axis=0)
    second = jnp.concatenate(second, axis=0)
    return dot_nt(first, b0) + dot_nt(second, b1)


def for_children(field, t):
    own = own_child()
    d = dot_nt(both_halves(field), t)
    return [
        jnp.where(own, jnp.concatenate([d[16 * k : 16 * k + 16]] * 8, axis=0), 0.0)
        for k in range(2)
    ]


def from_tops(ft, all_tops, tc, tm, b0, b1):
    w0, w1 = widen(0), widen(1)
    order = regroup()
    shape = (128, 128)
    fold = ones_where(iota(shape, 0) % 64 == iota(shape, 1) % 64)
    shape = (16, 128)
    half = iota(shape, 1) // 64
    found = []
    for n in range(32):
        top = ft[n // 16, n % 16]
        dev = top // 2
        y, x, z, c = dev // 32, (dev // 8) % 4, (dev // 2) % 4, dev % 2
        v = all_tops[c, y, z, x]
        found.append(jnp.where(half == top % 2, v, jnp.zeros_like(v)))
    found = dot(jnp.concatenate(found, axis=0), fold).astype(BF)
    fields = []
    for t in range(2):
        total = jnp.zeros((32, 32), F32)
        for jh in range(2):
            regrouped = dot(order, tc[t, jh * 256 : (jh + 1) * 256, :]).astype(BF)
            first = (t * 16 + jh * 8) * 16
            srcs = [both_halves(found[first + 16 * j : first + 16 * (j + 1)]) for j in range(8)]
            total = total + blocks_times(srcs, regrouped)
        total = total.astype(BF)
        fields.append((dot(total[:16], w0) + dot(total[16:], w1)).astype(BF))
    first, second = zip(*[for_children(fields[t], tm[t]) for t in range(2)])
    return converted([v.astype(BF) for v in first], [v.astype(BF) for v in second], b0, b1)


def from_mids(parts):
    wide = []
    for part in parts:
        total = part[0].astype(F32)
        for k in range(1, 4):
            total = total + part[k].astype(F32)
        wide.append(total)
    wide = jnp.concatenate(wide, axis=1).astype(BF)
    shape = (256, 16)
    repeat = ones_where(iota(shape, 0) // 16 == iota(shape, 1))
    shape = (256, 1024)
    keep = iota(shape, 1) % 16 == iota(shape, 0) % 16
    m = jnp.where(keep, dot(repeat, wide), 0.0).astype(BF)
    shape = (1024, 128)
    to_m = ones_where(iota(shape, 0) // 16 == iota(shape, 1) % 64)
    return dot(m, to_m)


def leaves_out(fields, tl, basis, near_part, far_part, b0, b1, out):
    own = own_child()
    shape = (64, 128)
    row, col = iota(shape, 0), iota(shape, 1)
    same = row % 8 == col // 16
    pick0 = ones_where(same & (col % 16 == 2 * (row // 8)))
    pick1 = ones_where(same & (col % 16 == 2 * (row // 8) + 1))
    low = low_lanes(shape)
    first, second = [], []
    for k in range(GROUPS):
        m0, m1 = for_children(fields[16 * k : 16 * k + 16], tl[k])
        first.append(m0.astype(BF))
        second.append(m1.astype(BF))
    leaf = (converted(first, second, b0, b1) + far_part).astype(BF)
    first, second = [], []
    for k in range(GROUPS):
        z = dot_nt(both_halves(leaf[128 * k : 128 * k + 128]), basis[k])
        first.append(jnp.where(own, z[:128], 0.0).astype(BF))
        second.append(jnp.where(own, z[128:], 0.0).astype(BF))
    total = (converted(first, second, b0, b1) + near_part).astype(BF)
    for k in range(GROUPS):
        v = total[128 * k : 128 * (k + 1)]
        out[k] = jnp.where(low, dot(pick0, v), dot(pick1, v))


def as_tiles(a):
    n = a.shape[0]
    return a.reshape(n, 8, 32, 128).transpose(0, 2, 1, 3).reshape(n, 256, 128)


VMEM = pl.BlockSpec(memory_space=pltpu.VMEM)
ANY = pl.BlockSpec(memory_space=pl.ANY)
SMEM = pl.BlockSpec(memory_space=pltpu.SMEM)
LIMIT = 56 * 1024 * 1024


def body(
    points,
    basis,
    transfer_leaf,
    transfer_mid,
    near_blocks,
    near_src,
    leaf_coupling,
    far_leaf,
    mid_coupling,
    mid_target,
    top_coupling,
    far_top,
):
    pt = points.reshape(16, 8, 8, 128).transpose(0, 2, 1, 3).reshape(16, 64, 128)
    bt = as_tiles(basis.reshape(16, 8, 4096))
    tl = as_tiles(transfer_leaf.reshape(16, 8, 4096))
    tm = as_tiles(transfer_mid.reshape(2, 8, 4096))
    cm = as_tiles(mid_coupling.reshape(32, 8, 4096)).reshape(16, 512, 128)
    tc = as_tiles(top_coupling.reshape(4, 8, 4096)).reshape(2, 512, 128)
    nb = as_tiles(near_blocks)
    fb = as_tiles(leaf_coupling)

    lanes = (384, 256, 384)
    out = pl.pallas_call(
        near_kernel,
        out_shape=jax.ShapeDtypeStruct((16, 64, 128), F32),
        in_specs=[SMEM] * 3 + [VMEM] + [ANY] * 8,
        out_specs=VMEM,
        scratch_shapes=[
            pltpu.VMEM((128, 256, 128), BF),
            pltpu.VMEM((128, 256, 128), BF),
            pltpu.VMEM((2048, 64), F32),
            pltpu.VMEM((2048, 64), F32),
            pltpu.VMEM((2048, 128), F32),
            pltpu.VMEM((2048, 128), F32),
            pltpu.VMEM((256, 128), F32),
            pltpu.VMEM((512, 16, 128), BF),
            pltpu.VMEM((512, 16, 128), BF),
            pltpu.VMEM((LEAVES, 256, 128), F32),
            pltpu.VMEM((2, 1024, 128), BF),
            pltpu.VMEM((2, 1024, 128), BF),
            pltpu.VMEM((2, 128, 256), BF),
            pltpu.VMEM((16, 512, 128), BF),
            pltpu.VMEM((8, 256, 128), BF),
            pltpu.VMEM((16, 64, 128), BF),
            pltpu.VMEM((16, 256, 128), BF),
            pltpu.VMEM((16, 256, 128), BF),
            pltpu.VMEM((2, 256, 128), BF),
            pltpu.VMEM((2, 512, 128), BF),
            pltpu.VMEM((1024, 128), BF),
            pltpu.VMEM((1024, 128), BF),
            pltpu.VMEM((256, 128), BF),
            pltpu.VMEM((16, 128), BF),
            pltpu.VMEM((2, 4, 4, 4, 16, 128), BF),
        ]
        + [pltpu.VMEM((8, n // 2 + 16, 128), BF) for n in lanes] * 2
        + [pltpu.VMEM((4, 64, n), BF) for n in lanes] * 2
        + [pltpu.VMEM((4, 16, n), BF) for n in lanes] * 2
        + [
            pltpu.SemaphoreType.DMA((53,)),
            pltpu.SemaphoreType.DMA((53,)),
            pltpu.SemaphoreType.DMA((13,)),
            pltpu.SemaphoreType.DMA((2 * STEPS,)),
        ],
        compiler_params=pltpu.CompilerParams(
            vmem_limit_bytes=LIMIT, collective_id=0, has_side_effects=True
        ),
        name="whole",
    )(near_src.T, far_leaf.T, far_top, mid_target, nb, fb, pt, bt, tl, tm, cm, tc)
    return out.astype(BF).reshape(16, 8, 8, 128).transpose(0, 2, 1, 3).reshape(128, 1024)


def solution(mesh):
    both = P(AXES, None)
    three = P(AXES, None, None)
    return jax.shard_map(
        body,
        mesh=mesh,
        in_specs=(
            both, both, both, both, three, both, three, both, three, both, three, both,
        ),
        out_specs=both,
        check_vma=False,
    )
```

```python
import functools

import jax
import jax.numpy as jnp
from jax import lax
from jax.experimental import pallas as pl
from jax.experimental.pallas import tpu as pltpu
from jax.sharding import PartitionSpec as P

F32 = jnp.float32
BF = jnp.bfloat16
AXES = ("grp", "dev")
GROUPS = 16
DEVICES = 128
LEAVES = 16
STEPS = 128 // LEAVES


def dot(a, b):
    return jnp.dot(a, b, preferred_element_type=F32)


def dot_nt(a, b):
    return lax.dot_general(a, b, (((1,), (1,)), ((), ())), preferred_element_type=F32)


def iota(shape, dim):
    return lax.broadcasted_iota(jnp.int32, shape, dim)


def ones_where(condition):
    return jnp.where(condition, 1.0, 0.0).astype(BF)


def low_lanes(shape):
    return iota(shape, len(shape) - 1) < 64


def spread(half):
    shape = (64, 256)
    return ones_where(iota(shape, 0) == 2 * (iota(shape, 1) // 8) + half)


def gather_back(half):
    shape = (128, 256)
    return ones_where(iota(shape, 0) % 64 == 2 * (iota(shape, 1) // 8) + half)


def own_child():
    shape = (128, 256)
    return iota(shape, 0) // 16 == iota(shape, 1) % 8


def fold_halves(first, second):
    v = jnp.where(low_lanes(first.shape), first, second)
    return v + pltpu.roll(v, 64, 1)


def both_halves(v):
    low = low_lanes(v.shape)
    zero = jnp.zeros_like(v)
    return jnp.concatenate([jnp.where(low, v, zero), jnp.where(low, zero, v)], axis=0)


def up_pass(loads, points_ready, coefs_ready, pt, basis, tl, tm, xp, cp, mc, tops, xd, cd, own_at):
    e01 = jnp.concatenate([spread(0), spread(1)], axis=1)
    shape = (2048, 512)
    own = (iota(shape, 0) // 16) % 8 == iota(shape, 1) % 8
    shape = (128, 64)
    pick = ones_where(
        (iota(shape, 0) // 16 == iota(shape, 1) % 8)
        & ((iota(shape, 0) % 16) // 2 == iota(shape, 1) // 8)
    )
    shape = (128, 128)
    fold = ones_where(iota(shape, 0) % 64 == iota(shape, 1) % 64)
    parity = iota(shape, 1) // 64 == iota(shape, 0) % 2

    def expanded(v):
        n = v.shape[0]
        return jnp.where(own[:n], dot(v[:, :64], e01), 0.0)

    def parents(v, blocks):
        n = len(blocks)
        lhs = jnp.sum(expanded(v).reshape(n, 8, 16, 512), axis=1).astype(BF)
        out = []
        for k in range(n):
            d = dot(jnp.concatenate([lhs[k, :, :256], lhs[k, :, 256:]], axis=0), blocks[k])
            out.append(fold_halves(d[:16], d[16:]).astype(BF))
        return jnp.concatenate(out, axis=0)

    loads[0].wait()
    a = [jnp.where(parity, dot(pick, pt[k]), 0.0).astype(BF) for k in range(GROUPS)]
    x = dot(jnp.concatenate(a, axis=0), fold).astype(BF)
    low = low_lanes((1024, 128))
    xp[...] = jnp.where(low, x[:1024], x[1024:])
    points_ready()
    at = pl.ds(pl.multiple_of(own_at, 128), 128)
    xd[at] = x.reshape(128, 16, 128)
    wide = expanded(x).astype(BF)
    loads[1].wait()
    coef = []
    for k in range(GROUPS):
        w = wide[128 * k : 128 * (k + 1)]
        c = dot(jnp.concatenate([w[:, :256], w[:, 256:]], axis=0), basis[k])
        coef.append(fold_halves(c[:128], c[128:]).astype(BF))
    coef = jnp.concatenate(coef, axis=0)
    cp[...] = jnp.where(low, coef[:1024], coef[1024:])
    coefs_ready()
    cd[at] = coef.reshape(128, 16, 128)
    loads[2].wait()
    mc[...] = parents(coef, [tl[k] for k in range(GROUPS)])
    loads[3].wait()
    both = parents(mc[...], [tm[0], tm[1]])
    tops[...] = jnp.where(low_lanes((16, 128)), both[:16], both[16:])


def regroup():
    shape = (256, 256)
    row, col = iota(shape, 0), iota(shape, 1)
    return ones_where((row // 32 == col % 8) & (row % 32 == col // 8))


def widen(half):
    shape = (32, 128)
    return ones_where(iota(shape, 1) % 64 == 2 * iota(shape, 0) + half)


def blocks_times(sources, regrouped):
    lhs = jnp.concatenate(sources, axis=1)
    rhs = jnp.concatenate([regrouped[32 * j : 32 * (j + 1)] for j in range(8)], axis=1)
    return dot_nt(lhs, rhs)


def place_messages(cm, mt, mc, msgs, cb, formed):
    rep = iota((8, 8, 128), 2) // 32

    def mid_step(s, carry):
        y = both_halves(mc[pl.ds(pl.multiple_of(s * 16, 16), 16), :])
        y = jnp.concatenate([y] * 4, axis=0)
        zero = jnp.zeros_like(y)
        top = jnp.concatenate([y, zero], axis=1)
        low = jnp.concatenate([zero, y], axis=1)
        block = jnp.concatenate([cm[s, 0:256, :], cm[s, 256:512, :]], axis=1)
        r = dot_nt(block, jnp.concatenate([top, low], axis=0))
        parts = []
        for jh in range(2):
            b = r[:, 128 * jh : 128 * jh + 128].reshape(8, 4, 8, 128)
            q = b[:, 0]
            for k in range(1, 4):
                q = jnp.where(rep == k, b[:, k], q)
            parts.append(q)
        cb[:, pl.ds(pl.multiple_of(s * 16, 16), 16), :] = jnp.concatenate(parts, axis=1).astype(BF)
        return carry

    lax.fori_loop(0, GROUPS, mid_step, 0, unroll=4)

    target = mt[...]
    owner = target // 16
    parts = (owner // 32, (owner // 8) % 4, (owner // 2) % 4, owner % 2, target % 16)
    parts = jnp.concatenate(parts, axis=0).astype(F32).astype(BF)
    shape = (16, 256)
    along = ones_where(iota(shape, 1) % 16 == iota(shape, 0))
    mine = iota(shape, 1) // 16 == iota(shape, 0)
    parts = dot(parts, along)
    y, x, z, c, local = [
        jnp.sum(jnp.where(mine, parts[16 * k : 16 * k + 16], 0.0), axis=0, keepdims=True)
        for k in range(5)
    ]
    shape = (128, 256)
    onehot = iota(shape, 0).astype(F32) == 32.0 * y + 8.0 * x + 2.0 * z + c
    shape = (256, 256)
    earlier = ones_where(iota(shape, 0) < iota(shape, 1))
    rank = jnp.where(onehot, dot(ones_where(onehot), earlier), 0.0)
    rank = jnp.sum(rank, axis=0, keepdims=True)

    plans = (
        (0, 3, 2.0 * x + c, 4.0 * z + y),
        (3, 2, 2.0 * z + c, 4.0 * y + x),
        (5, 3, 2.0 * y + c, 4.0 * x + z),
    )
    for n, (first, count, stop, rest) in enumerate(plans):
        msg = msgs[n]
        at = 4.0 * rest + rank
        slot = iota((512, 256), 0).astype(F32)
        place = ones_where(slot == 64.0 * stop + at)
        wide = jnp.concatenate([cb[first + k] for k in range(count)], axis=1)
        wide = dot(place, wide).astype(BF)
        for k in range(count):
            rows = wide[:, 128 * k : 128 * k + 128].reshape(8, 64, 128)
            msg[:, 64 * k : 64 * k + 64, :] = rows
        shape = (128, 256)
        to_stop = (iota(shape, 0) // 16).astype(F32) == stop
        value = jnp.where(to_stop, local + 1.0, 0.0).astype(BF)
        lane = ones_where((iota(shape, 0) % 64).astype(F32) == at)
        label = dot_nt(value, lane) - 1.0
        msg[:, 64 * count : 64 * count + 16, :] = label.astype(BF).reshape(8, 16, 128)
        formed(n)


def sum_messages(count, landed, sums):
    shape = (16, 128)
    first = iota(shape, 1) < 64
    labels = pl.ds(64 * count, 16)
    lab = [
        jnp.where(first, landed[2 * q, labels, :], landed[2 * q + 1, labels, :])
        for q in range(4)
    ]
    lab = jnp.concatenate(lab, axis=1).astype(F32)
    shape = (16, 512)
    hit = lab == iota(shape, 0).astype(F32)
    to = (iota(shape, 1) // 4) % 16
    lhs = jnp.concatenate([ones_where(hit & (to == n)) for n in range(16)], axis=0)
    parts = [landed[:, 64 * k : 64 * k + 64, :].reshape(512, 128) for k in range(count)]
    total = dot(lhs, jnp.concatenate(parts, axis=1)).astype(BF)
    sums[...] = total.reshape(4, 64, 128 * count)


def near_kernel(
    near_idx, far_idx, ft, mt, near_in, far_in, pt_in, basis_in, tl_in, tm_in, cm_in, tc_in,
    out,
    near, far, near_sum, far_sum, near_part, far_part, down, xd, cd, stage, xland, cland, bw, cm, cb, pt, basis, tl, tm, tc, xp, cp, mc, tops,
    all_tops,
    msg_a, msg_b, msg_c, land_a, land_b, land_c,
    sum_a, sum_b, sum_c, next_a, next_b, next_c, part_a, part_b, part_c,
    sums_a, sums_b, sums_c, send, recv, here, fetch,
):
    y = lax.axis_index("grp")
    dev = lax.axis_index("dev")
    x, z, c = dev // 8, (dev // 2) % 4, dev % 2
    me = y * 32 + dev
    right = lax.rem(me + 1, DEVICES)
    left = lax.rem(me + DEVICES - 1, DEVICES)
    mesh = pl.DeviceIdType.MESH

    def remote(src, dst, n, device):
        return pltpu.make_async_remote_copy(
            src_ref=src,
            dst_ref=dst,
            send_sem=send.at[n],
            recv_sem=recv.at[n],
            device_id=device,
            device_id_type=mesh,
        )

    def at_x(k):
        return (y, lax.rem(x + k, 4) * 8 + z * 2 + c)

    def at_y(k):
        return (lax.rem(y + k, 4), dev)

    def at_z(k):
        return (y, x * 8 + lax.rem(z + k, 4) * 2 + c)

    def at_xc(k):
        m = lax.rem(x * 2 + c + k, 8)
        return (y, (m // 2) * 8 + z * 2 + m % 2)

    def at_yc(k):
        m = lax.rem(y * 2 + c + k, 8)
        return (m // 2, x * 8 + z * 2 + m % 2)

    def at_zc(k):
        return (y, x * 8 + lax.rem(z * 2 + c + k, 8))

    def halos(n):
        src, dst = ((xp, xland), (cp, cland))[n]
        return [
            remote(src, dst.at[k], 2 * n + k, (to // 32, to % 32))
            for k, to in enumerate((right, left))
        ]

    def tops_to(n):
        if n == 0:
            return [remote(tops, all_tops.at[c, y, z, x], 3 + k, at_x(k)) for k in range(1, 4)]
        if n == 1:
            block = all_tops.at[c, y, z]
            return [remote(block, block, 6 + k, at_z(k)) for k in range(1, 4)]
        if n == 2:
            block = all_tops.at[c, y]
            return [remote(block, block, 9 + k, at_y(k)) for k in range(1, 4)]
        block = all_tops.at[c]
        return [remote(block, block, 13, (y, x * 8 + z * 2 + 1 - c))]

    plans = (
        (3, (x, z, y), (at_xc, at_z, at_y), msg_a, land_a, sum_a, next_a, part_a, sums_a),
        (2, (z, y, x), (at_zc, at_y, at_x), msg_b, land_b, sum_b, next_b, part_b, sums_b),
        (3, (y, x, z), (at_yc, at_x, at_z), msg_c, land_c, sum_c, next_c, part_c, sums_c),
    )

    def first_hop(n):
        _, (a, _, _), (to, _, _), msg, land = plans[n][:5]
        own = a * 2 + c
        return [
            remote(msg.at[lax.rem(own + k, 8)], land.at[own], 13 + 7 * n + k, to(k))
            for k in range(1, 8)
        ]

    def second_hop(n):
        _, (_, a, _), (_, to, _), _, _, src, dst = plans[n][:7]
        return [
            remote(src.at[lax.rem(a + k, 4)], dst.at[a], 34 + 3 * n + k, to(k))
            for k in range(1, 4)
        ]

    def third_hop(n):
        _, (_, _, a), (_, _, to), _, _, _, _, src, dst = plans[n]
        return [
            remote(src.at[lax.rem(a + k, 4)], dst.at[a], 43 + 3 * n + k, to(k))
            for k in range(1, 4)
        ]

    def own_first(n):
        own = plans[n][1][0] * 2 + c
        return pltpu.make_async_copy(plans[n][3].at[own], plans[n][4].at[own], here.at[n])

    def own_third(n):
        own = plans[n][1][2]
        return pltpu.make_async_copy(plans[n][7].at[own], plans[n][8].at[own], here.at[3 + n])

    def own_tops():
        return pltpu.make_async_copy(tops, all_tops.at[c, y, z, x], here.at[6])

    def chunk(src, dst, base, n):
        part = pl.ds(n * LEAVES, LEAVES)
        return pltpu.make_async_copy(src.at[part], dst.at[part], fetch.at[base + n])

    def start(copies):
        for copy in copies:
            copy.start()

    def arrive(copies):
        for copy in copies:
            copy.wait_recv()

    low = low_lanes((1024, 128))

    def unpack(dst, part, n):
        shape = (128, 128)
        swap = ones_where((iota(shape, 0) + 64) % 128 == iota(shape, 1))
        v = part[...]
        w = dot(v, swap).astype(BF)
        for h, (lo, hi) in enumerate(((v, w), (w, v))):
            at = pl.ds(pl.multiple_of((dev + n) % 4 * 128 + h * 64, 64), 64)
            dst[at] = jnp.where(low, lo, hi).reshape(64, 16, 128)

    pairs = (
        (pt_in, pt), (basis_in, basis), (tl_in, tl), (tm_in, tm), (cm_in, cm), (tc_in, tc),
    )
    loads = [
        pltpu.make_async_copy(src, dst, here.at[7 + n]) for n, (src, dst) in enumerate(pairs)
    ]
    start(loads)
    barrier = pltpu.get_barrier_semaphore()

    def greet(device):
        pl.semaphore_signal(barrier, inc=1, device_id=device, device_id_type=mesh)

    for to in (right, left):
        greet((to // 32, to % 32))
    for k in range(1, 8):
        greet(at_xc(k))
        greet(at_yc(k))
        greet(at_zc(k))

    def points_ready():
        pl.semaphore_wait(barrier, 23)
        start(halos(0))
        start([chunk(near_in, near, 0, n) for n in range(STEPS)])

    def coefs_ready():
        start(halos(1))
        start([chunk(far_in, far, STEPS, n) for n in range(STEPS)])

    up_pass(loads, points_ready, coefs_ready, pt, basis, tl, tm, xp, cp, mc, tops, xd, cd, dev % 4 * 128)
    start(tops_to(0))
    own_tops().start()
    loads[4].wait()
    loads[5].wait()

    def formed(n):
        start(first_hop(n))
        own_first(n).start()

    place_messages(cm, mt, mc, (msg_a, msg_b, msg_c), cb, formed)
    bw[0] = gather_back(0)
    bw[1] = gather_back(1)
    arrive(halos(0))
    unpack(xd, xland.at[0], 3)
    unpack(xd, xland.at[1], 1)

    def work(g, idx, blocks, src, out):
        low_f = low_lanes((32, 128))
        low_x = low_lanes((16, 128))
        for i in range(LEAVES):
            at = g * LEAVES + i
            plane = stage.at[i]
            plane[...] = blocks[at].astype(F32)
            found = [src[idx[j, at] & 511] for j in range(8)]
            lhs, first, second = [], [], []
            for j in range(0, 8, 2):
                lhs.append(jnp.where(low_x, found[j], found[j + 1]))
                even = plane[pl.ds(j, 32, stride=8), :]
                odd = plane[pl.ds(j + 1, 32, stride=8), :]
                turned = pltpu.roll(jnp.where(low_f, odd, even), 64, 1)
                first.append(jnp.where(low_f, even, turned).astype(BF))
                second.append(jnp.where(low_f, turned, odd).astype(BF))
            rhs = [jnp.concatenate(v, axis=1) for v in (first, second)]
            o = dot_nt(jnp.concatenate(lhs, axis=1), jnp.concatenate(rhs, axis=0))
            rows = pl.ds(pl.multiple_of(at * 16, 16), 16)
            out[rows, :] = o

    def near_step(g, carry):
        @pl.when(g == 1)
        def _():
            own_tops().wait()
            arrive(tops_to(0))
            start(tops_to(1))

        chunk(near_in, near, 0, g).wait()
        work(g, near_idx, near, xd, near_sum)
        return carry

    lax.fori_loop(0, STEPS, near_step, 0)
    arrive(halos(1))
    unpack(cd, cland.at[0], 3)
    unpack(cd, cland.at[1], 1)

    def far_step(g, carry):
        @pl.when(g == 2)
        def _():
            for n in range(3):
                own_first(n).wait()
                arrive(first_hop(n))
            for n in range(3):
                sum_messages(plans[n][0], plans[n][4], plans[n][5])
            for n in range(3):
                start(second_hop(n))
            arrive(tops_to(1))
            start(tops_to(2))

        @pl.when(g == STEPS - 1)
        def _():
            for n in range(3):
                arrive(second_hop(n))
            for n in range(3):
                at, own, got, dst = plans[n][1][1], plans[n][5], plans[n][6], plans[n][7]
                total = own[at].astype(F32)
                for k in range(1, 4):
                    total = total + got[lax.rem(at + k, 4)].astype(F32)
                dst[...] = total.astype(BF).reshape(dst.shape)
            for n in range(3):
                start(third_hop(n))
                own_third(n).start()
            arrive(tops_to(2))
            start(tops_to(3))

        chunk(far_in, far, STEPS, g).wait()
        work(g, far_idx, far, cd, far_sum)
        return carry

    lax.fori_loop(0, STEPS, far_step, 0)
    b0, b1 = bw[0], bw[1]
    shape = (64, 128)
    row = iota(shape, 0)
    in_order = ones_where(iota(shape, 1) % 64 == 2 * (row % 32) + row // 32)
    near_part[...] = dot(near_sum[...].astype(BF), in_order)
    far_part[...] = dot(far_sum[...].astype(BF), in_order)
    arrive(tops_to(3))
    down[...] = from_tops(ft, all_tops, tc, tm, b0, b1)
    for n in range(3):
        own_third(n).wait()
        arrive(third_hop(n))
    fields = (from_mids((sums_a, sums_b, sums_c)) + down[...]).astype(BF)
    leaves_out(fields, tl, basis, near_part[...], far_part[...], b0, b1, out)
    sent = [halos(0), halos(1)] + [tops_to(n) for n in range(4)]
    for n in range(3):
        sent += [first_hop(n), second_hop(n), third_hop(n)]
    for copies in sent:
        for copy in copies:
            copy.wait_send()


def converted(first, second, b0, b1):
    first = jnp.concatenate(first, axis=0)
    second = jnp.concatenate(second, axis=0)
    return dot_nt(first, b0) + dot_nt(second, b1)


def for_children(field, t):
    own = own_child()
    d = dot_nt(both_halves(field), t)
    return [
        jnp.where(own, jnp.concatenate([d[16 * k : 16 * k + 16]] * 8, axis=0), 0.0)
        for k in range(2)
    ]


def from_tops(ft, all_tops, tc, tm, b0, b1):
    w0, w1 = widen(0), widen(1)
    order = regroup()
    shape = (128, 128)
    fold = ones_where(iota(shape, 0) % 64 == iota(shape, 1) % 64)
    shape = (16, 128)
    half = iota(shape, 1) // 64
    found = []
    for n in range(32):
        top = ft[n // 16, n % 16]
        dev = top // 2
        y, x, z, c = dev // 32, (dev // 8) % 4, (dev // 2) % 4, dev % 2
        v = all_tops[c, y, z, x]
        found.append(jnp.where(half == top % 2, v, jnp.zeros_like(v)))
    found = dot(jnp.concatenate(found, axis=0), fold).astype(BF)
    fields = []
    for t in range(2):
        total = jnp.zeros((32, 32), F32)
        for jh in range(2):
            regrouped = dot(order, tc[t, jh * 256 : (jh + 1) * 256, :]).astype(BF)
            first = (t * 16 + jh * 8) * 16
            srcs = [both_halves(found[first + 16 * j : first + 16 * (j + 1)]) for j in range(8)]
            total = total + blocks_times(srcs, regrouped)
        total = total.astype(BF)
        fields.append((dot(total[:16], w0) + dot(total[16:], w1)).astype(BF))
    first, second = zip(*[for_children(fields[t], tm[t]) for t in range(2)])
    return converted([v.astype(BF) for v in first], [v.astype(BF) for v in second], b0, b1)


def from_mids(parts):
    wide = []
    for part in parts:
        total = part[0].astype(F32)
        for k in range(1, 4):
            total = total + part[k].astype(F32)
        wide.append(total)
    wide = jnp.concatenate(wide, axis=1).astype(BF)
    shape = (256, 16)
    repeat = ones_where(iota(shape, 0) // 16 == iota(shape, 1))
    shape = (256, 1024)
    keep = iota(shape, 1) % 16 == iota(shape, 0) % 16
    m = jnp.where(keep, dot(repeat, wide), 0.0).astype(BF)
    shape = (1024, 128)
    to_m = ones_where(iota(shape, 0) // 16 == iota(shape, 1) % 64)
    return dot(m, to_m)


def leaves_out(fields, tl, basis, near_part, far_part, b0, b1, out):
    own = own_child()
    shape = (64, 128)
    row, col = iota(shape, 0), iota(shape, 1)
    same = row % 8 == col // 16
    pick0 = ones_where(same & (col % 16 == 2 * (row // 8)))
    pick1 = ones_where(same & (col % 16 == 2 * (row // 8) + 1))
    low = low_lanes(shape)
    first, second = [], []
    for k in range(GROUPS):
        m0, m1 = for_children(fields[16 * k : 16 * k + 16], tl[k])
        first.append(m0.astype(BF))
        second.append(m1.astype(BF))
    leaf = (converted(first, second, b0, b1) + far_part).astype(BF)
    first, second = [], []
    for k in range(GROUPS):
        z = dot_nt(both_halves(leaf[128 * k : 128 * k + 128]), basis[k])
        first.append(jnp.where(own, z[:128], 0.0).astype(BF))
        second.append(jnp.where(own, z[128:], 0.0).astype(BF))
    total = (converted(first, second, b0, b1) + near_part).astype(BF)
    for k in range(GROUPS):
        v = total[128 * k : 128 * (k + 1)]
        out[k] = jnp.where(low, dot(pick0, v), dot(pick1, v)).astype(BF)


def as_tiles(a):
    n = a.shape[0]
    return a.reshape(n, 8, 32, 128).transpose(0, 2, 1, 3).reshape(n, 256, 128)


VMEM = pl.BlockSpec(memory_space=pltpu.VMEM)
ANY = pl.BlockSpec(memory_space=pl.ANY)
SMEM = pl.BlockSpec(memory_space=pltpu.SMEM)
LIMIT = 56 * 1024 * 1024


def body(
    points,
    basis,
    transfer_leaf,
    transfer_mid,
    near_blocks,
    near_src,
    leaf_coupling,
    far_leaf,
    mid_coupling,
    mid_target,
    top_coupling,
    far_top,
):
    pt = points.reshape(16, 8, 8, 128).transpose(0, 2, 1, 3).reshape(16, 64, 128)
    bt = as_tiles(basis.reshape(16, 8, 4096))
    tl = as_tiles(transfer_leaf.reshape(16, 8, 4096))
    tm = as_tiles(transfer_mid.reshape(2, 8, 4096))
    cm = as_tiles(mid_coupling.reshape(32, 8, 4096)).reshape(16, 512, 128)
    tc = as_tiles(top_coupling.reshape(4, 8, 4096)).reshape(2, 512, 128)
    nb = as_tiles(near_blocks)
    fb = as_tiles(leaf_coupling)

    lanes = (384, 256, 384)
    out = pl.pallas_call(
        near_kernel,
        out_shape=jax.ShapeDtypeStruct((16, 64, 128), BF),
        in_specs=[SMEM] * 3 + [VMEM] + [ANY] * 8,
        out_specs=VMEM,
        scratch_shapes=[
            pltpu.VMEM((128, 256, 128), BF),
            pltpu.VMEM((128, 256, 128), BF),
            pltpu.VMEM((2048, 64), F32),
            pltpu.VMEM((2048, 64), F32),
            pltpu.VMEM((2048, 128), F32),
            pltpu.VMEM((2048, 128), F32),
            pltpu.VMEM((256, 128), F32),
            pltpu.VMEM((512, 16, 128), BF),
            pltpu.VMEM((512, 16, 128), BF),
            pltpu.VMEM((LEAVES, 256, 128), F32),
            pltpu.VMEM((2, 1024, 128), BF),
            pltpu.VMEM((2, 1024, 128), BF),
            pltpu.VMEM((2, 128, 256), BF),
            pltpu.VMEM((16, 512, 128), BF),
            pltpu.VMEM((8, 256, 128), BF),
            pltpu.VMEM((16, 64, 128), BF),
            pltpu.VMEM((16, 256, 128), BF),
            pltpu.VMEM((16, 256, 128), BF),
            pltpu.VMEM((2, 256, 128), BF),
            pltpu.VMEM((2, 512, 128), BF),
            pltpu.VMEM((1024, 128), BF),
            pltpu.VMEM((1024, 128), BF),
            pltpu.VMEM((256, 128), BF),
            pltpu.VMEM((16, 128), BF),
            pltpu.VMEM((2, 4, 4, 4, 16, 128), BF),
        ]
        + [pltpu.VMEM((8, n // 2 + 16, 128), BF) for n in lanes] * 2
        + [pltpu.VMEM((4, 64, n), BF) for n in lanes] * 2
        + [pltpu.VMEM((4, 16, n), BF) for n in lanes] * 2
        + [
            pltpu.SemaphoreType.DMA((53,)),
            pltpu.SemaphoreType.DMA((53,)),
            pltpu.SemaphoreType.DMA((13,)),
            pltpu.SemaphoreType.DMA((2 * STEPS,)),
        ],
        compiler_params=pltpu.CompilerParams(
            vmem_limit_bytes=LIMIT, collective_id=0, has_side_effects=True
        ),
        name="whole",
    )(near_src.T, far_leaf.T, far_top, mid_target, nb, fb, pt, bt, tl, tm, cm, tc)
    return out.reshape(16, 8, 8, 128).transpose(0, 2, 1, 3).reshape(128, 1024)


def solution(mesh):
    both = P(AXES, None)
    three = P(AXES, None, None)
    return jax.shard_map(
        body,
        mesh=mesh,
        in_specs=(
            both, both, both, both, three, both, three, both, three, both, three, both,
        ),
        out_specs=both,
        check_vma=False,
    )
```

```python
import functools

import jax
import jax.numpy as jnp
from jax import lax
from jax.experimental import pallas as pl
from jax.experimental.pallas import tpu as pltpu
from jax.sharding import PartitionSpec as P

F32 = jnp.float32
BF = jnp.bfloat16
AXES = ("grp", "dev")
GROUPS = 16
DEVICES = 128
LEAVES = 16
STEPS = 128 // LEAVES


def dot(a, b):
    return jnp.dot(a, b, preferred_element_type=F32)


def dot_nt(a, b):
    return lax.dot_general(a, b, (((1,), (1,)), ((), ())), preferred_element_type=F32)


def iota(shape, dim):
    return lax.broadcasted_iota(jnp.int32, shape, dim)


def ones_where(condition):
    return jnp.where(condition, 1.0, 0.0).astype(BF)


def low_lanes(shape):
    return iota(shape, len(shape) - 1) < 64


def spread(half):
    shape = (64, 256)
    return ones_where(iota(shape, 0) == 2 * (iota(shape, 1) // 8) + half)


def gather_back(half):
    shape = (128, 256)
    return ones_where(iota(shape, 0) % 64 == 2 * (iota(shape, 1) // 8) + half)


def own_child():
    shape = (128, 256)
    return iota(shape, 0) // 16 == iota(shape, 1) % 8


def fold_halves(first, second):
    v = jnp.where(low_lanes(first.shape), first, second)
    return v + pltpu.roll(v, 64, 1)


def both_halves(v):
    low = low_lanes(v.shape)
    zero = jnp.zeros_like(v)
    return jnp.concatenate([jnp.where(low, v, zero), jnp.where(low, zero, v)], axis=0)


def up_pass(loads, points_ready, coefs_ready, pt, basis, tl, tm, xp, cp, mc, tops, xd, cd, own_at):
    e01 = jnp.concatenate([spread(0), spread(1)], axis=1)
    shape = (2048, 512)
    own = (iota(shape, 0) // 16) % 8 == iota(shape, 1) % 8
    shape = (128, 64)
    pick = ones_where(
        (iota(shape, 0) // 16 == iota(shape, 1) % 8)
        & ((iota(shape, 0) % 16) // 2 == iota(shape, 1) // 8)
    )
    shape = (128, 128)
    fold = ones_where(iota(shape, 0) % 64 == iota(shape, 1) % 64)
    parity = iota(shape, 1) // 64 == iota(shape, 0) % 2

    def expanded(v):
        n = v.shape[0]
        return jnp.where(own[:n], dot(v[:, :64], e01), 0.0)

    def parents(v, blocks):
        n = len(blocks)
        lhs = jnp.sum(expanded(v).reshape(n, 8, 16, 512), axis=1).astype(BF)
        out = []
        for k in range(n):
            d = dot(jnp.concatenate([lhs[k, :, :256], lhs[k, :, 256:]], axis=0), blocks[k])
            out.append(fold_halves(d[:16], d[16:]).astype(BF))
        return jnp.concatenate(out, axis=0)

    loads[0].wait()
    a = [jnp.where(parity, dot(pick, pt[k]), 0.0).astype(BF) for k in range(GROUPS)]
    x = dot(jnp.concatenate(a, axis=0), fold).astype(BF)
    low = low_lanes((1024, 128))
    xp[...] = jnp.where(low, x[:1024], x[1024:])
    points_ready()
    at = pl.ds(pl.multiple_of(own_at, 128), 128)
    xd[at] = x.reshape(128, 16, 128)
    wide = expanded(x).astype(BF)
    loads[1].wait()
    coef = []
    for k in range(GROUPS):
        w = wide[128 * k : 128 * (k + 1)]
        c = dot(jnp.concatenate([w[:, :256], w[:, 256:]], axis=0), basis[k])
        coef.append(fold_halves(c[:128], c[128:]).astype(BF))
    coef = jnp.concatenate(coef, axis=0)
    cp[...] = jnp.where(low, coef[:1024], coef[1024:])
    coefs_ready()
    cd[at] = coef.reshape(128, 16, 128)
    loads[2].wait()
    mc[...] = parents(coef, [tl[k] for k in range(GROUPS)])
    loads[3].wait()
    both = parents(mc[...], [tm[0], tm[1]])
    tops[...] = jnp.where(low_lanes((16, 128)), both[:16], both[16:])


def regroup():
    shape = (256, 256)
    row, col = iota(shape, 0), iota(shape, 1)
    return ones_where((row // 32 == col % 8) & (row % 32 == col // 8))


def widen(half):
    shape = (32, 128)
    return ones_where(iota(shape, 1) % 64 == 2 * iota(shape, 0) + half)


def blocks_times(sources, regrouped):
    lhs = jnp.concatenate(sources, axis=1)
    rhs = jnp.concatenate([regrouped[32 * j : 32 * (j + 1)] for j in range(8)], axis=1)
    return dot_nt(lhs, rhs)


def place_messages(cm, mt, mc, msgs, cb, formed):
    rep = iota((8, 8, 128), 2) // 32

    def mid_step(s, carry):
        y = both_halves(mc[pl.ds(pl.multiple_of(s * 16, 16), 16), :])
        y = jnp.concatenate([y] * 4, axis=0)
        zero = jnp.zeros_like(y)
        top = jnp.concatenate([y, zero], axis=1)
        low = jnp.concatenate([zero, y], axis=1)
        block = jnp.concatenate([cm[s, 0:256, :], cm[s, 256:512, :]], axis=1)
        r = dot_nt(block, jnp.concatenate([top, low], axis=0))
        parts = []
        for jh in range(2):
            b = r[:, 128 * jh : 128 * jh + 128].reshape(8, 4, 8, 128)
            q = b[:, 0]
            for k in range(1, 4):
                q = jnp.where(rep == k, b[:, k], q)
            parts.append(q)
        cb[:, pl.ds(pl.multiple_of(s * 16, 16), 16), :] = jnp.concatenate(parts, axis=1).astype(BF)
        return carry

    lax.fori_loop(0, GROUPS, mid_step, 0, unroll=4)

    target = mt[...]
    owner = target // 16
    parts = (owner // 32, (owner // 8) % 4, (owner // 2) % 4, owner % 2, target % 16)
    parts = jnp.concatenate(parts, axis=0).astype(F32).astype(BF)
    shape = (16, 256)
    along = ones_where(iota(shape, 1) % 16 == iota(shape, 0))
    mine = iota(shape, 1) // 16 == iota(shape, 0)
    parts = dot(parts, along)
    y, x, z, c, local = [
        jnp.sum(jnp.where(mine, parts[16 * k : 16 * k + 16], 0.0), axis=0, keepdims=True)
        for k in range(5)
    ]
    shape = (128, 256)
    onehot = iota(shape, 0).astype(F32) == 32.0 * y + 8.0 * x + 2.0 * z + c
    shape = (256, 256)
    earlier = ones_where(iota(shape, 0) < iota(shape, 1))
    rank = jnp.where(onehot, dot(ones_where(onehot), earlier), 0.0)
    rank = jnp.sum(rank, axis=0, keepdims=True)

    plans = (
        (0, 2, 2.0 * x + c, 4.0 * z + y),
        (2, 2, 2.0 * z + c, 4.0 * y + x),
        (4, 4, 2.0 * y + c, 4.0 * x + z),
    )
    for n, (first, count, stop, rest) in enumerate(plans):
        msg = msgs[n]
        at = 4.0 * rest + rank
        slot = iota((512, 256), 0).astype(F32)
        place = ones_where(slot == 64.0 * stop + at)
        wide = jnp.concatenate([cb[first + k] for k in range(count)], axis=1)
        wide = dot(place, wide).astype(BF)
        for k in range(count):
            rows = wide[:, 128 * k : 128 * k + 128].reshape(8, 64, 128)
            msg[:, 64 * k : 64 * k + 64, :] = rows
        shape = (128, 256)
        to_stop = (iota(shape, 0) // 16).astype(F32) == stop
        value = jnp.where(to_stop, local + 1.0, 0.0).astype(BF)
        lane = ones_where((iota(shape, 0) % 64).astype(F32) == at)
        label = dot_nt(value, lane) - 1.0
        msg[:, 64 * count : 64 * count + 16, :] = label.astype(BF).reshape(8, 16, 128)
        formed(n)


def sum_messages(count, landed, sums):
    shape = (16, 128)
    first = iota(shape, 1) < 64
    labels = pl.ds(64 * count, 16)
    lab = [
        jnp.where(first, landed[2 * q, labels, :], landed[2 * q + 1, labels, :])
        for q in range(4)
    ]
    lab = jnp.concatenate(lab, axis=1).astype(F32)
    shape = (16, 512)
    hit = lab == iota(shape, 0).astype(F32)
    to = (iota(shape, 1) // 4) % 16
    lhs = jnp.concatenate([ones_where(hit & (to == n)) for n in range(16)], axis=0)
    parts = [landed[:, 64 * k : 64 * k + 64, :].reshape(512, 128) for k in range(count)]
    total = dot(lhs, jnp.concatenate(parts, axis=1)).astype(BF)
    sums[...] = total.reshape(4, 64, 128 * count)


def near_kernel(
    near_idx, far_idx, ft, mt, near_in, far_in, pt_in, basis_in, tl_in, tm_in, cm_in, tc_in,
    out,
    near, far, near_sum, far_sum, near_part, far_part, down, xd, cd, stage, xland, cland, bw, cm, cb, pt, basis, tl, tm, tc, xp, cp, mc, tops,
    all_tops,
    msg_a, msg_b, msg_c, land_a, land_b, land_c,
    sum_a, sum_b, sum_c, next_a, next_b, next_c, part_a, part_b, part_c,
    sums_a, sums_b, sums_c, send, recv, here, fetch,
):
    y = lax.axis_index("grp")
    dev = lax.axis_index("dev")
    x, z, c = dev // 8, (dev // 2) % 4, dev % 2
    me = y * 32 + dev
    right = lax.rem(me + 1, DEVICES)
    left = lax.rem(me + DEVICES - 1, DEVICES)
    mesh = pl.DeviceIdType.MESH

    def remote(src, dst, n, device):
        return pltpu.make_async_remote_copy(
            src_ref=src,
            dst_ref=dst,
            send_sem=send.at[n],
            recv_sem=recv.at[n],
            device_id=device,
            device_id_type=mesh,
        )

    def at_x(k):
        return (y, lax.rem(x + k, 4) * 8 + z * 2 + c)

    def at_y(k):
        return (lax.rem(y + k, 4), dev)

    def at_z(k):
        return (y, x * 8 + lax.rem(z + k, 4) * 2 + c)

    def at_xc(k):
        m = lax.rem(x * 2 + c + k, 8)
        return (y, (m // 2) * 8 + z * 2 + m % 2)

    def at_yc(k):
        m = lax.rem(y * 2 + c + k, 8)
        return (m // 2, x * 8 + z * 2 + m % 2)

    def at_zc(k):
        return (y, x * 8 + lax.rem(z * 2 + c + k, 8))

    def halos(n):
        src, dst = ((xp, xland), (cp, cland))[n]
        return [
            remote(src, dst.at[k], 2 * n + k, (to // 32, to % 32))
            for k, to in enumerate((right, left))
        ]

    def tops_to(n):
        if n == 0:
            return [remote(tops, all_tops.at[c, y, z, x], 3 + k, at_x(k)) for k in range(1, 4)]
        if n == 1:
            block = all_tops.at[c, y, z]
            return [remote(block, block, 6 + k, at_z(k)) for k in range(1, 4)]
        if n == 2:
            block = all_tops.at[c, y]
            return [remote(block, block, 9 + k, at_y(k)) for k in range(1, 4)]
        block = all_tops.at[c]
        return [remote(block, block, 13, (y, x * 8 + z * 2 + 1 - c))]

    plans = (
        (2, (x, z, y), (at_xc, at_z, at_y), msg_a, land_a, sum_a, next_a, part_a, sums_a),
        (2, (z, y, x), (at_zc, at_y, at_x), msg_b, land_b, sum_b, next_b, part_b, sums_b),
        (4, (y, x, z), (at_yc, at_x, at_z), msg_c, land_c, sum_c, next_c, part_c, sums_c),
    )

    def first_hop(n):
        _, (a, _, _), (to, _, _), msg, land = plans[n][:5]
        own = a * 2 + c
        return [
            remote(msg.at[lax.rem(own + k, 8)], land.at[own], 13 + 7 * n + k, to(k))
            for k in range(1, 8)
        ]

    def second_hop(n):
        _, (_, a, _), (_, to, _), _, _, src, dst = plans[n][:7]
        return [
            remote(src.at[lax.rem(a + k, 4)], dst.at[a], 34 + 3 * n + k, to(k))
            for k in range(1, 4)
        ]

    def third_hop(n):
        _, (_, _, a), (_, _, to), _, _, _, _, src, dst = plans[n]
        return [
            remote(src.at[lax.rem(a + k, 4)], dst.at[a], 43 + 3 * n + k, to(k))
            for k in range(1, 4)
        ]

    def own_first(n):
        own = plans[n][1][0] * 2 + c
        return pltpu.make_async_copy(plans[n][3].at[own], plans[n][4].at[own], here.at[n])

    def own_third(n):
        own = plans[n][1][2]
        return pltpu.make_async_copy(plans[n][7].at[own], plans[n][8].at[own], here.at[3 + n])

    def own_tops():
        return pltpu.make_async_copy(tops, all_tops.at[c, y, z, x], here.at[6])

    def chunk(src, dst, base, n):
        part = pl.ds(n * LEAVES, LEAVES)
        return pltpu.make_async_copy(src.at[part], dst.at[part], fetch.at[base + n])

    def start(copies):
        for copy in copies:
            copy.start()

    def arrive(copies):
        for copy in copies:
            copy.wait_recv()

    low = low_lanes((1024, 128))

    def unpack(dst, part, n):
        shape = (128, 128)
        swap = ones_where((iota(shape, 0) + 64) % 128 == iota(shape, 1))
        v = part[...]
        w = dot(v, swap).astype(BF)
        for h, (lo, hi) in enumerate(((v, w), (w, v))):
            at = pl.ds(pl.multiple_of((dev + n) % 4 * 128 + h * 64, 64), 64)
            dst[at] = jnp.where(low, lo, hi).reshape(64, 16, 128)

    pairs = (
        (pt_in, pt), (basis_in, basis), (tl_in, tl), (tm_in, tm), (cm_in, cm), (tc_in, tc),
    )
    loads = [
        pltpu.make_async_copy(src, dst, here.at[7 + n]) for n, (src, dst) in enumerate(pairs)
    ]
    start(loads)
    barrier = pltpu.get_barrier_semaphore()

    def greet(device):
        pl.semaphore_signal(barrier, inc=1, device_id=device, device_id_type=mesh)

    for to in (right, left):
        greet((to // 32, to % 32))
    for k in range(1, 8):
        greet(at_xc(k))
        greet(at_yc(k))
        greet(at_zc(k))

    def points_ready():
        pl.semaphore_wait(barrier, 23)
        start(halos(0))
        start([chunk(near_in, near, 0, n) for n in range(STEPS)])

    def coefs_ready():
        start(halos(1))
        start([chunk(far_in, far, STEPS, n) for n in range(STEPS)])

    up_pass(loads, points_ready, coefs_ready, pt, basis, tl, tm, xp, cp, mc, tops, xd, cd, dev % 4 * 128)
    start(tops_to(0))
    own_tops().start()
    loads[4].wait()
    loads[5].wait()

    def formed(n):
        start(first_hop(n))
        own_first(n).start()

    place_messages(cm, mt, mc, (msg_a, msg_b, msg_c), cb, formed)
    bw[0] = gather_back(0)
    bw[1] = gather_back(1)
    arrive(halos(0))
    unpack(xd, xland.at[0], 3)
    unpack(xd, xland.at[1], 1)

    def work(g, idx, blocks, src, out):
        low_f = low_lanes((32, 128))
        low_x = low_lanes((16, 128))
        for i in range(LEAVES):
            at = g * LEAVES + i
            plane = stage.at[i]
            plane[...] = blocks[at].astype(F32)
            found = [src[idx[j, at] & 511] for j in range(8)]
            lhs, first, second = [], [], []
            for j in range(0, 8, 2):
                lhs.append(jnp.where(low_x, found[j], found[j + 1]))
                even = plane[pl.ds(j, 32, stride=8), :]
                odd = plane[pl.ds(j + 1, 32, stride=8), :]
                turned = pltpu.roll(jnp.where(low_f, odd, even), 64, 1)
                first.append(jnp.where(low_f, even, turned).astype(BF))
                second.append(jnp.where(low_f, turned, odd).astype(BF))
            rhs = [jnp.concatenate(v, axis=1) for v in (first, second)]
            o = dot_nt(jnp.concatenate(lhs, axis=1), jnp.concatenate(rhs, axis=0))
            rows = pl.ds(pl.multiple_of(at * 16, 16), 16)
            out[rows, :] = o

    def near_step(g, carry):
        @pl.when(g == 1)
        def _():
            own_tops().wait()
            arrive(tops_to(0))
            start(tops_to(1))

        chunk(near_in, near, 0, g).wait()
        work(g, near_idx, near, xd, near_sum)
        return carry

    lax.fori_loop(0, STEPS, near_step, 0)
    arrive(halos(1))
    unpack(cd, cland.at[0], 3)
    unpack(cd, cland.at[1], 1)

    def far_step(g, carry):
        @pl.when(g == 2)
        def _():
            for n in range(3):
                own_first(n).wait()
                arrive(first_hop(n))
            for n in range(3):
                sum_messages(plans[n][0], plans[n][4], plans[n][5])
            for n in range(3):
                start(second_hop(n))
            arrive(tops_to(1))
            start(tops_to(2))

        @pl.when(g == STEPS - 1)
        def _():
            for n in range(3):
                arrive(second_hop(n))
            for n in range(3):
                at, own, got, dst = plans[n][1][1], plans[n][5], plans[n][6], plans[n][7]
                total = own[at].astype(F32)
                for k in range(1, 4):
                    total = total + got[lax.rem(at + k, 4)].astype(F32)
                dst[...] = total.astype(BF).reshape(dst.shape)
            for n in range(3):
                start(third_hop(n))
                own_third(n).start()
            arrive(tops_to(2))
            start(tops_to(3))

        chunk(far_in, far, STEPS, g).wait()
        work(g, far_idx, far, cd, far_sum)
        return carry

    lax.fori_loop(0, STEPS, far_step, 0)
    b0, b1 = bw[0], bw[1]
    shape = (64, 128)
    row = iota(shape, 0)
    in_order = ones_where(iota(shape, 1) % 64 == 2 * (row % 32) + row // 32)
    near_part[...] = dot(near_sum[...].astype(BF), in_order)
    far_part[...] = dot(far_sum[...].astype(BF), in_order)
    arrive(tops_to(3))
    down[...] = from_tops(ft, all_tops, tc, tm, b0, b1)
    for n in range(3):
        own_third(n).wait()
        arrive(third_hop(n))
    fields = (from_mids((sums_a, sums_b, sums_c)) + down[...]).astype(BF)
    leaves_out(fields, tl, basis, near_part[...], far_part[...], b0, b1, out)
    sent = [halos(0), halos(1)] + [tops_to(n) for n in range(4)]
    for n in range(3):
        sent += [first_hop(n), second_hop(n), third_hop(n)]
    for copies in sent:
        for copy in copies:
            copy.wait_send()


def converted(first, second, b0, b1):
    first = jnp.concatenate(first, axis=0)
    second = jnp.concatenate(second, axis=0)
    return dot_nt(first, b0) + dot_nt(second, b1)


def for_children(field, t):
    own = own_child()
    d = dot_nt(both_halves(field), t)
    return [
        jnp.where(own, jnp.concatenate([d[16 * k : 16 * k + 16]] * 8, axis=0), 0.0)
        for k in range(2)
    ]


def from_tops(ft, all_tops, tc, tm, b0, b1):
    w0, w1 = widen(0), widen(1)
    order = regroup()
    shape = (128, 128)
    fold = ones_where(iota(shape, 0) % 64 == iota(shape, 1) % 64)
    shape = (16, 128)
    half = iota(shape, 1) // 64
    found = []
    for n in range(32):
        top = ft[n // 16, n % 16]
        dev = top // 2
        y, x, z, c = dev // 32, (dev // 8) % 4, (dev // 2) % 4, dev % 2
        v = all_tops[c, y, z, x]
        found.append(jnp.where(half == top % 2, v, jnp.zeros_like(v)))
    found = dot(jnp.concatenate(found, axis=0), fold).astype(BF)
    fields = []
    for t in range(2):
        total = jnp.zeros((32, 32), F32)
        for jh in range(2):
            regrouped = dot(order, tc[t, jh * 256 : (jh + 1) * 256, :]).astype(BF)
            first = (t * 16 + jh * 8) * 16
            srcs = [both_halves(found[first + 16 * j : first + 16 * (j + 1)]) for j in range(8)]
            total = total + blocks_times(srcs, regrouped)
        total = total.astype(BF)
        fields.append((dot(total[:16], w0) + dot(total[16:], w1)).astype(BF))
    first, second = zip(*[for_children(fields[t], tm[t]) for t in range(2)])
    return converted([v.astype(BF) for v in first], [v.astype(BF) for v in second], b0, b1)


def from_mids(parts):
    wide = []
    for part in parts:
        total = part[0].astype(F32)
        for k in range(1, 4):
            total = total + part[k].astype(F32)
        wide.append(total)
    wide = jnp.concatenate(wide, axis=1).astype(BF)
    shape = (256, 16)
    repeat = ones_where(iota(shape, 0) // 16 == iota(shape, 1))
    shape = (256, 1024)
    keep = iota(shape, 1) % 16 == iota(shape, 0) % 16
    m = jnp.where(keep, dot(repeat, wide), 0.0).astype(BF)
    shape = (1024, 128)
    to_m = ones_where(iota(shape, 0) // 16 == iota(shape, 1) % 64)
    return dot(m, to_m)


def leaves_out(fields, tl, basis, near_part, far_part, b0, b1, out):
    own = own_child()
    shape = (64, 128)
    row, col = iota(shape, 0), iota(shape, 1)
    same = row % 8 == col // 16
    pick0 = ones_where(same & (col % 16 == 2 * (row // 8)))
    pick1 = ones_where(same & (col % 16 == 2 * (row // 8) + 1))
    low = low_lanes(shape)
    first, second = [], []
    for k in range(GROUPS):
        m0, m1 = for_children(fields[16 * k : 16 * k + 16], tl[k])
        first.append(m0.astype(BF))
        second.append(m1.astype(BF))
    leaf = (converted(first, second, b0, b1) + far_part).astype(BF)
    first, second = [], []
    for k in range(GROUPS):
        z = dot_nt(both_halves(leaf[128 * k : 128 * k + 128]), basis[k])
        first.append(jnp.where(own, z[:128], 0.0).astype(BF))
        second.append(jnp.where(own, z[128:], 0.0).astype(BF))
    total = (converted(first, second, b0, b1) + near_part).astype(BF)
    for k in range(GROUPS):
        v = total[128 * k : 128 * (k + 1)]
        out[k] = jnp.where(low, dot(pick0, v), dot(pick1, v)).astype(BF)


def as_tiles(a):
    n = a.shape[0]
    return a.reshape(n, 8, 32, 128).transpose(0, 2, 1, 3).reshape(n, 256, 128)


VMEM = pl.BlockSpec(memory_space=pltpu.VMEM)
ANY = pl.BlockSpec(memory_space=pl.ANY)
SMEM = pl.BlockSpec(memory_space=pltpu.SMEM)
LIMIT = 56 * 1024 * 1024


def body(
    points,
    basis,
    transfer_leaf,
    transfer_mid,
    near_blocks,
    near_src,
    leaf_coupling,
    far_leaf,
    mid_coupling,
    mid_target,
    top_coupling,
    far_top,
):
    pt = points.reshape(16, 8, 8, 128).transpose(0, 2, 1, 3).reshape(16, 64, 128)
    bt = as_tiles(basis.reshape(16, 8, 4096))
    tl = as_tiles(transfer_leaf.reshape(16, 8, 4096))
    tm = as_tiles(transfer_mid.reshape(2, 8, 4096))
    cm = as_tiles(mid_coupling.reshape(32, 8, 4096)).reshape(16, 512, 128)
    tc = as_tiles(top_coupling.reshape(4, 8, 4096)).reshape(2, 512, 128)
    nb = as_tiles(near_blocks)
    fb = as_tiles(leaf_coupling)

    lanes = (256, 256, 512)
    out = pl.pallas_call(
        near_kernel,
        out_shape=jax.ShapeDtypeStruct((16, 64, 128), BF),
        in_specs=[SMEM] * 3 + [VMEM] + [ANY] * 8,
        out_specs=VMEM,
        scratch_shapes=[
            pltpu.VMEM((128, 256, 128), BF),
            pltpu.VMEM((128, 256, 128), BF),
            pltpu.VMEM((2048, 64), F32),
            pltpu.VMEM((2048, 64), F32),
            pltpu.VMEM((2048, 128), F32),
            pltpu.VMEM((2048, 128), F32),
            pltpu.VMEM((256, 128), F32),
            pltpu.VMEM((512, 16, 128), BF),
            pltpu.VMEM((512, 16, 128), BF),
            pltpu.VMEM((LEAVES, 256, 128), F32),
            pltpu.VMEM((2, 1024, 128), BF),
            pltpu.VMEM((2, 1024, 128), BF),
            pltpu.VMEM((2, 128, 256), BF),
            pltpu.VMEM((16, 512, 128), BF),
            pltpu.VMEM((8, 256, 128), BF),
            pltpu.VMEM((16, 64, 128), BF),
            pltpu.VMEM((16, 256, 128), BF),
            pltpu.VMEM((16, 256, 128), BF),
            pltpu.VMEM((2, 256, 128), BF),
            pltpu.VMEM((2, 512, 128), BF),
            pltpu.VMEM((1024, 128), BF),
            pltpu.VMEM((1024, 128), BF),
            pltpu.VMEM((256, 128), BF),
            pltpu.VMEM((16, 128), BF),
            pltpu.VMEM((2, 4, 4, 4, 16, 128), BF),
        ]
        + [pltpu.VMEM((8, n // 2 + 16, 128), BF) for n in lanes] * 2
        + [pltpu.VMEM((4, 64, n), BF) for n in lanes] * 2
        + [pltpu.VMEM((4, 16, n), BF) for n in lanes] * 2
        + [
            pltpu.SemaphoreType.DMA((53,)),
            pltpu.SemaphoreType.DMA((53,)),
            pltpu.SemaphoreType.DMA((13,)),
            pltpu.SemaphoreType.DMA((2 * STEPS,)),
        ],
        compiler_params=pltpu.CompilerParams(
            vmem_limit_bytes=LIMIT, collective_id=0, has_side_effects=True
        ),
        name="whole",
    )(near_src.T, far_leaf.T, far_top, mid_target, nb, fb, pt, bt, tl, tm, cm, tc)
    return out.reshape(16, 8, 8, 128).transpose(0, 2, 1, 3).reshape(128, 1024)


def solution(mesh):
    both = P(AXES, None)
    three = P(AXES, None, None)
    return jax.shard_map(
        body,
        mesh=mesh,
        in_specs=(
            both, both, both, both, three, both, three, both, three, both, three, both,
        ),
        out_specs=both,
        check_vma=False,
    )
```
